512 devices in a mesh: blk: 8 (over y_hi, core), grp: 64 (over y_lo, x, z).
Axes of the slice: x: 4, y: 8 (y_hi: 4, y_lo: 2; y = y_hi * 2 + y_lo), z: 8, core: 2. Of those that a mesh axis runs over, the one named last changes fastest.
Arguments:
- patches: bfloat16 [393216, 1152], P(('blk', 'grp')), may hold values from -6 to 6
- segment_ids: int32 [512, 768], P(('blk', 'grp')), may hold values from 0 to 2, never falling along the last dimension, each value on 1 to 512 neighbouring positions
- image_ids: int32 [1536], P(('blk', 'grp')), may hold values from 0 to 1535, each once
- text_embeds: bfloat16 [1536, 1152], P(('blk', 'grp')), may hold values from -6 to 6
- key_weight: bfloat16 [1152, 1152], P('grp'), may hold values from -0.1875 to 0.1875
- value_weight: bfloat16 [1152, 1152], P('grp'), may hold values from -0.1875 to 0.1875
- pool_query: bfloat16 [1152], replicated, may hold values from -110 to 110
- logit_scale: float32 [1], replicated, may hold values from 90 to 110
- logit_bias: float32 [1], replicated, may hold values from -9 to -7
Outputs:
- image_grad: float32 [1536, 1152], P(('blk', 'grp'))
- text_grad: float32 [1536, 1152], P(('blk', 'grp'))
The draws below stay inside these ranges and needn't reach their ends.
Inputs may be any that keep to these rules, and one draw needn't show every extreme that they name: `segment_ids`: the rows of each image slot of a device form one run; every slot holds at least one row and one slot of every device exactly 512. `image_ids`: every pair index appears exactly once.
All inputs are finite; a program needn't handle non-finite values.
Results may differ from the reference program's by a relative error of at most 0.018.
The reference program's roundings to bfloat16 on the way (of `key_rows`, `value_rows`, `weights`, `image_low`, `text_low` and `scaled`) count: a program that leaves them out, or rounds other values in their place, can miss the bound.
Values may be sent and summed in bfloat16 or wider, within the bound.
No kernel may reach another device: no remote copies, remote signals or barrier semaphores. Data moves between devices by JAX's collectives and lax.ppermute only.
A program may use at most 64 MiB of HBM per device.

```python
import math
import jax
import jax.numpy as jnp
import numpy as np
from jax import lax

D = 1152
HEADS = 16
HEAD_DIM = 72
ROWS_DEV = 768
IMG_DEV = 3
PAIRS = 1536
ALL_ROWS = 393216
DEVICES = 512


def draw_pool_query(key, part):
    key = jax.random.fold_in(key, 7)
    values = 2.0 * jnp.clip(jax.random.normal(key, (D,), jnp.float32), -4.0, 4.0)
    return values.astype(jnp.bfloat16)


def steps_of(key, extent, shards, low, top_value):
    factor_of, own = 1.0, jax.random.fold_in(key, 6)
    for position, shards_of in shards:
        heights = jnp.exp(jax.random.uniform(jax.random.fold_in(own, position), (shards_of,), jnp.float32, low / len(shards), top_value / len(shards)))
        factor_of = factor_of * jnp.repeat(heights, extent[position] // shards_of).reshape([-1 if axis == position else 1 for axis in range(len(extent))])
    return factor_of


def length_profile(amount, total, most, skew):
    weights = [(1 << 20) // math.isqrt(standing ** skew) + 1 for standing in range(2, amount + 1)]
    surplus, holding = total - most - (amount - 1), [1] * (amount - 1)
    while surplus > 0:
        candidates = [i for i in range(amount - 1) if holding[i] < most]
        whole, left = sum([weights[i] for i in candidates]), surplus
        for i in candidates:
            more = min(most - holding[i], max(1, left * weights[i] // whole), surplus)
            holding[i] = holding[i] + more
            surplus = surplus - more
    return np.array([most] + holding)


def ragged(key, amount, total, limit, slope):
    if amount == 2:
        one = jax.random.randint(key, (), max(1, total - limit), min(limit, total - 1) + 1)
        return jnp.stack([one, total - one])
    lengths = jnp.asarray(length_profile(amount, total, limit, slope), jnp.int32)
    twos = (amount - 1) // 2
    giver, sink = lengths[1:1 + 2 * twos:2], lengths[2:2 + 2 * twos:2]
    slack = jnp.minimum(giver - 1, limit - sink)
    moved = jax.random.randint(jax.random.fold_in(key, 1), (twos,), 0, 1 << 20) % (slack + 1)
    lengths = lengths.at[1:1 + 2 * twos:2].set(giver - moved).at[2:2 + 2 * twos:2].set(sink + moved)
    return lengths[jax.random.permutation(jax.random.fold_in(key, 2), amount)]


def centred(key, shape, width, most, cuts=(), held_as=jnp.bfloat16):
    array = width * jax.random.normal(key, shape, jnp.float32)
    if cuts:
        array = array * steps_of(key, shape, cuts, -0.22, 0.18)
    return jnp.clip(array, -most, most).astype(held_as)


def setup_inputs(seed: int = 0) -> dict:
    arg_keys = jax.random.split(jax.random.key(seed), 10)
    patches = centred(arg_keys[0], (ALL_ROWS, D), 1.0, 6.0, ((0, 512),))
    segment_ids = jax.vmap(lambda own: jnp.searchsorted(jnp.cumsum(ragged(own, IMG_DEV, ROWS_DEV, ROWS_DEV * 2 // 3, 2)), jnp.arange(ROWS_DEV), side="right"))(jax.random.split(arg_keys[1], DEVICES)).reshape((DEVICES, ROWS_DEV)).astype(jnp.int32)
    image_ids = jax.random.permutation(arg_keys[2], PAIRS).astype(jnp.int32)
    text_embeds = centred(arg_keys[3], (PAIRS, D), 1.0, 6.0, ((0, 512),))
    key_weight = centred(arg_keys[4], (D, D), D ** -0.5, 0.1875, ((0, 64),))
    value_weight = centred(arg_keys[5], (D, D), D ** -0.5, 0.1875, ((0, 64),))
    pool_query = draw_pool_query(jax.random.fold_in(arg_keys[9], 71), 0)
    logit_scale = jnp.clip(jax.random.uniform(arg_keys[7], (1,), jnp.float32, 90.0, 110.0), 90.0, 110.0)
    logit_bias = jnp.clip(jax.random.uniform(arg_keys[8], (1,), jnp.float32, -9.0, -7.0), -9.0, -7.0)
    return dict(patches=patches, segment_ids=segment_ids, image_ids=image_ids, text_embeds=text_embeds, key_weight=key_weight, value_weight=value_weight, pool_query=pool_query, logit_scale=logit_scale, logit_bias=logit_bias)


def pool_device(patch_rows, segment_row, key_weight, value_weight, pool_query):
    key_rows = jnp.dot(patch_rows, key_weight, preferred_element_type=jnp.float32).astype(jnp.bfloat16)
    value_rows = jnp.dot(patch_rows, value_weight, preferred_element_type=jnp.float32).astype(jnp.bfloat16)
    row_count = patch_rows.shape[0]
    query = pool_query.astype(jnp.float32).reshape(HEADS, HEAD_DIM)
    scores = jnp.einsum('rhe,he->rh', key_rows.astype(jnp.float32).reshape(row_count, HEADS, HEAD_DIM), query) / math.sqrt(HEAD_DIM)
    slot_mask = segment_row[None, :] == jnp.arange(IMG_DEV, dtype=jnp.int32)[:, None]
    masked = jnp.where(slot_mask[:, :, None], scores[None, :, :], -1e+30)
    peak_score = lax.optimization_barrier(jnp.max(masked, axis=1, keepdims=True))
    powers = jnp.where(slot_mask[:, :, None], jnp.exp(masked - peak_score), 0.0)
    weights = (powers / lax.optimization_barrier(jnp.sum(powers, axis=1, keepdims=True))).astype(jnp.bfloat16)
    pooled = jnp.einsum('srh,rhe->she', weights.astype(jnp.float32), value_rows.astype(jnp.float32).reshape(row_count, HEADS, HEAD_DIM))
    return pooled.reshape(IMG_DEV, D)

def reference(patches, segment_ids, image_ids, text_embeds, key_weight, value_weight, pool_query, logit_scale, logit_bias):
    blocks = patches.reshape(DEVICES, ROWS_DEV, D)

    def one_device(pair):
        return pool_device(pair[0], pair[1], key_weight, value_weight, pool_query)
    pooled = lax.map(one_device, (blocks, segment_ids)).reshape(PAIRS, D)
    image_norm = jnp.sqrt(lax.optimization_barrier(jnp.sum(pooled * pooled, axis=1, keepdims=True)) + 1e-06)
    unit_image = pooled / image_norm
    image_low = unit_image.astype(jnp.bfloat16)
    text_full = text_embeds.astype(jnp.float32)
    text_norm = jnp.sqrt(lax.optimization_barrier(jnp.sum(text_full * text_full, axis=1, keepdims=True)) + 1e-06)
    unit_text = text_full / text_norm
    text_low = unit_text.astype(jnp.bfloat16)
    scale = logit_scale[0]
    logits = scale * jnp.dot(image_low, text_low.T, preferred_element_type=jnp.float32) + logit_bias[0]
    pair_sign = jnp.where(image_ids[:, None] == jnp.arange(PAIRS, dtype=jnp.int32)[None, :], 1.0, -1.0)
    scaled = (scale * (-pair_sign * jax.nn.sigmoid(-pair_sign * logits) / PAIRS)).astype(jnp.bfloat16)
    image_part = jnp.dot(scaled, text_low, preferred_element_type=jnp.float32)
    text_part = jnp.dot(scaled.T, image_low, preferred_element_type=jnp.float32)
    image_grad = (image_part - unit_image * lax.optimization_barrier(jnp.sum(unit_image * image_part, axis=1, keepdims=True))) / image_norm
    text_grad = (text_part - unit_text * lax.optimization_barrier(jnp.sum(unit_text * text_part, axis=1, keepdims=True))) / text_norm
    return (image_grad, text_grad)
```

```python
import math

import jax
import jax.numpy as jnp
from jax import lax
from jax.experimental import pallas as pl
from jax.experimental.pallas import tpu as pltpu
from jax.sharding import Mesh
from jax.sharding import PartitionSpec as P

D = 1152
TILES = D // 128
HEADS = 16
HEAD_DIM = 72
IMG_DEV = 3
PAIRS = 1536
EPS = 1e-06
ID_BASE = 64
ROWS = 768
LOW = -1e30

FINE = ("yh", "core", "yl", "x", "z")
FINE_SHAPE = (4, 2, 2, 4, 8)
SIDE = ("core", "yl", "x")
FAR = ("yh", "z")
GRP = ("yl", "x", "z")
N_SIDE = 16
N_FAR = 32
N_GRP = 64
W_ROWS = 18

AT_FOLDED = HEAD_DIM
AT_KEY = AT_FOLDED + HEADS
KEY_FIRST = 128 - AT_KEY
KEY_REST = HEAD_DIM - KEY_FIRST

TOPS = 2
AT_TOP = IMG_DEV
AT_TEXT = AT_TOP + TOPS * IMG_DEV
AT_ID = AT_TEXT + IMG_DEV
AT_SCALAR = AT_ID + 1
N_LANES = 8

f32 = jnp.float32
bf16 = jnp.bfloat16
VMEM = pl.BlockSpec(memory_space=pltpu.VMEM)
SMEM = pl.BlockSpec(memory_space=pltpu.SMEM)


def call(kernel, outs, scratch=(), **cost):
    many = len(outs) > 1
    return pl.pallas_call(
        kernel,
        out_shape=tuple(outs) if many else outs[0],
        out_specs=(VMEM,) * len(outs) if many else VMEM,
        scratch_shapes=list(scratch),
        compiler_params=pltpu.CompilerParams(vmem_limit_bytes=40 * 1024 * 1024),
        **cost,
    )


def shape(*dims, dtype=f32):
    return jax.ShapeDtypeStruct(dims, dtype)


def iota(dims, axis):
    return lax.broadcasted_iota(jnp.int32, dims, axis)


def dot_nt(a, b):
    return lax.dot_general(a, b, (((1,), (1,)), ((), ())), preferred_element_type=f32)


def dot(a, b):
    return jnp.dot(a, b, preferred_element_type=f32)


def exchange(blocks, axes):
    return lax.all_to_all(blocks, axes, 0, 0)


def weight_kernel(core_ref, key_ref, value_ref, query_ref, out_ref, tile):
    keys = key_ref[...].astype(f32)
    values = value_ref[...].astype(f32)
    products = keys * query_ref[...].astype(f32)
    high = products.astype(bf16)
    low = (products - high.astype(f32)).astype(bf16)
    members = jnp.where(iota((HEADS, D), 1) // HEAD_DIM == iota((HEADS, D), 0), 1.0, 0.0).astype(bf16)
    folded = (dot_nt(high, members) + dot_nt(low, members)) * (1.0 / math.sqrt(HEAD_DIM))
    mine = core_ref[0] == 0
    half = HEADS // 2 * HEAD_DIM
    keys = jnp.where(mine, keys[:, :half], keys[:, half:])
    values = jnp.where(mine, values[:, :half], values[:, half:])
    tile[...] = jnp.zeros_like(tile)
    for head in range(HEADS // 2):
        at = head * HEAD_DIM
        tile[:W_ROWS, :HEAD_DIM] = values[:, at : at + HEAD_DIM]
        tile[:W_ROWS, AT_FOLDED:AT_KEY] = folded
        tile[:W_ROWS, AT_KEY:] = keys[:, at : at + KEY_FIRST]
        for part in range(3):
            tile[W_ROWS:, part * KEY_REST : (part + 1) * KEY_REST] = keys[
                part * 6 : part * 6 + 6, at + KEY_FIRST : at + HEAD_DIM
            ]
        out_ref[head * 8 : head * 8 + 8] = jnp.broadcast_to(tile[...].astype(bf16)[None], (8, 24, 128))


def three_parts(value):
    first = value.astype(bf16).astype(f32)
    rest = value - first
    second = rest.astype(bf16).astype(f32)
    return first, second, rest - second


def context_kernel(weights_ref, patches_ref, segments_ref, tail_ref, out_ref, pair_ref, main, extra, rows, marks):
    for source in range(N_GRP):
        block = weights_ref[source].astype(f32)
        at = source * W_ROWS
        main[at : at + W_ROWS, :] = block[:W_ROWS]
        for part in range(3):
            extra[at + part * 6 : at + part * 6 + 6, :] = block[
                W_ROWS:, part * KEY_REST : (part + 1) * KEY_REST
            ]
    packed = main[...]
    pair_ref[...] = jnp.concatenate([packed, packed[:, AT_KEY:], extra[...]], axis=1).astype(bf16)
    scores = dot(patches_ref[...], packed.astype(bf16)).T[AT_FOLDED:AT_KEY]

    place = iota((HEADS, ROWS), 1)
    lanes = iota((HEADS, 128), 1)
    marks[...] = jnp.zeros_like(marks)
    rows[...] = jnp.zeros_like(rows)
    scalars = jnp.zeros((HEADS, 128), f32)

    def put(row, value):
        for tile in range(ROWS // 128):
            rows[tile, pl.ds(row, HEADS, stride=16), :] = value[:, tile * 128 : (tile + 1) * 128]

    for slot in range(IMG_DEV):
        masked = jnp.where(segments_ref[...] == slot, scores, LOW)
        peak = jnp.max(masked, axis=1, keepdims=True)
        powers = jnp.where(masked > 0.5 * LOW, jnp.exp(masked - peak), 0.0)
        total = jnp.sum(powers, axis=1, keepdims=True)
        best = peak
        values = []
        for top in range(TOPS):
            if top > 0:
                best = jnp.max(masked, axis=1, keepdims=True)
            there = best > 0.5 * LOW
            first = jnp.min(jnp.where(masked == best, place, ROWS), axis=1, keepdims=True)
            hit = (place == first) & there
            put(AT_TOP + slot * TOPS + top, jnp.where(hit, 1.0, 0.0))
            masked = jnp.where(hit, LOW, masked)
            powers = jnp.where(hit, 0.0, powers)
            values.append(jnp.where(there, 1.0, 0.0))
        others = powers / total
        put(slot, others)
        values = [
            *three_parts(peak + jnp.log(total)),
            *three_parts(jnp.sum(others, axis=1, keepdims=True)),
            *values,
        ]
        for index, value in enumerate(values):
            scalars = jnp.where(lanes == slot * N_LANES + index, value, scalars)
    marks[pl.ds(AT_SCALAR, HEADS, stride=16), :] = scalars
    picks = jnp.concatenate([rows[tile].astype(bf16) for tile in range(ROWS // 128)], axis=1)
    context = dot(picks, patches_ref[...])
    context = context.reshape(HEADS, 16, D) + tail_ref[...].astype(f32)[None]
    out_ref[:, :, 128:] = context[:, :, 128:].astype(bf16)
    out_ref[:, :, :128] = (context[:, :, :128] + marks[...].reshape(HEADS, 16, 128)).astype(bf16)


def project_kernel(near_ref, pair_ref, query_ref, out_ref, value_rows, key_rows):
    near = near_ref[...].reshape(N_SIDE * 16, D)
    both = dot(near, pair_ref[...])
    value_rows[...] = both[:, :128]
    key_rows[:, :HEAD_DIM] = both[:, 128:]
    pick = jnp.where(iota((N_SIDE, N_SIDE * 16), 1) == iota((N_SIDE, N_SIDE * 16), 0) * 16 + AT_SCALAR, 1.0, 0.0)
    scalars = dot(pick.astype(bf16), near[:, :128])
    query = query_ref[...]
    pooled = []
    for slot in range(IMG_DEV):
        at = slot * N_LANES
        level = scalars[:, at : at + 1] + scalars[:, at + 1 : at + 2] + scalars[:, at + 2 : at + 3]
        others = scalars[:, at + 3 : at + 4] + scalars[:, at + 4 : at + 5] + scalars[:, at + 5 : at + 6]
        some = others > 0.0
        peak = jnp.where(some, 0.0, LOW)
        powers, values = [], []
        for top in range(TOPS):
            at_row = pl.ds(AT_TOP + slot * TOPS + top, N_SIDE, stride=16)
            keys = key_rows[at_row, :][:, :HEAD_DIM].astype(bf16).astype(f32)
            score = jnp.sum(keys * query, axis=1, keepdims=True) / math.sqrt(HEAD_DIM)
            there = scalars[:, at + 6 + top : at + 7 + top] > 0.5
            score = jnp.where(there, score - level, LOW)
            peak = jnp.maximum(peak, score)
            powers.append((there, score))
            values.append(value_rows[at_row, :][:, :HEAD_DIM].astype(bf16).astype(f32))
        powers = [jnp.where(there, jnp.exp(score - peak), 0.0) for there, score in powers]
        shift = jnp.where(some, jnp.exp(jnp.where(some, -peak, 0.0)), 0.0)
        total = others * shift
        for power in powers:
            total = total + power
        result = value_rows[pl.ds(slot, N_SIDE, stride=16), :][:, :HEAD_DIM] * (shift / total)
        for power, value in zip(powers, values):
            result = result + (power / total).astype(bf16).astype(f32) * value
        pooled.append(result)
    out_ref[...] = jnp.broadcast_to(jnp.concatenate(pooled, axis=1)[None], out_ref.shape)


def unit_kernel(side_ref, pooled_ref, tail_ref, out_ref, low_ref, unit_ref, norm_ref, units, norms, block):
    side = side_ref[0]
    for slot in range(IMG_DEV):
        for head in range(HEADS):
            units[slot, :, head * HEAD_DIM : (head + 1) * HEAD_DIM] = pooled_ref[
                head, :, slot * HEAD_DIM : (slot + 1) * HEAD_DIM
            ]
    block[...] = tail_ref[...].astype(f32)
    for slot in range(IMG_DEV):
        pooled = units[slot]
        norm = jnp.sqrt(jnp.sum(pooled * pooled, axis=1, keepdims=True) + EPS)
        unit = pooled / norm
        units[slot] = unit
        norms[slot] = jnp.broadcast_to(norm, (N_SIDE, 128))
        low_ref[slot * N_SIDE : (slot + 1) * N_SIDE, :] = unit.astype(bf16)
        own = units[slot, pl.ds(side, 1), :]
        block[slot : slot + 1, :] = own
        unit_ref[slot : slot + 1, :] = own
        norm_ref[slot : slot + 1, :] = norms[slot, pl.ds(side, 1), :]
    out_ref[...] = jnp.broadcast_to(block[...].astype(bf16)[None], out_ref.shape)


def pair_kernel(params_ref, side_ref, far_ref, text_ref, low_ref, index_ref, out_ref):
    scale, offset = params_ref[0], params_ref[1]
    side = side_ref[0]
    far = far_ref[...].reshape(N_FAR * 8, D)
    near = jnp.concatenate([text_ref[...], low_ref[...]], axis=0)
    digit = iota((8, 128), 1)
    slot = iota((8, 128), 0)
    code = jnp.where(digit == slot, float(ID_BASE), 0.0) + jnp.where(digit == slot + IMG_DEV, 1.0, 0.0)
    code = jnp.where(slot < IMG_DEV, code, 0.0).astype(bf16)
    ids = dot_nt(code, far[:, :128])
    columns = N_FAR * 8
    column = iota((1, columns), 1)
    kind = column % 8
    device = column // 8
    index = ((device // 8) * N_SIDE + side) * 8 + device % 8
    index = index * IMG_DEV + kind - IMG_DEV
    for position in range(IMG_DEV):
        moved = pltpu.roll(ids, columns - (6 - position), 1)[position : position + 1]
        index = jnp.where(kind == position, moved.astype(jnp.int32), index)
    logits = scale * dot_nt(near, far) + offset
    pair_sign = jnp.where(index_ref[...] == index, 1.0, -1.0)
    scaled = scale * (-pair_sign * jax.nn.sigmoid(-pair_sign * logits) / PAIRS)
    wanted = iota((6 * N_SIDE, columns), 0) // (IMG_DEV * N_SIDE)
    scaled = jnp.where(kind // IMG_DEV == wanted, scaled, 0.0).astype(bf16)
    parts = dot(scaled, far)
    for tile in range(TILES):
        for row in range(6):
            out_ref[:, tile * 6 + row, :] = parts[
                row * N_SIDE : (row + 1) * N_SIDE, tile * 128 : (tile + 1) * 128
            ]


def final_kernel(parts_ref, unit_text_ref, text_norm_ref, unit_image_ref, image_norm_ref, image_ref, text_ref, sums):
    total = parts_ref[0]
    for source in range(1, N_SIDE):
        total = total + parts_ref[source]
    sums[...] = total
    whole = jnp.concatenate([sums[tile * 6 : tile * 6 + 6, :] for tile in range(TILES)], axis=1)
    for first, unit_ref, norm, out_ref in (
        (0, unit_text_ref, text_norm_ref[...], text_ref),
        (IMG_DEV, unit_image_ref, image_norm_ref[:, :1], image_ref),
    ):
        part = whole[first : first + IMG_DEV]
        unit = unit_ref[...]
        out_ref[...] = (part - unit * jnp.sum(unit * part, axis=1, keepdims=True)) / norm


def code_ids(ids):
    row = jnp.concatenate([ids // ID_BASE, ids % ID_BASE]).astype(bf16)
    return jnp.pad(row, (0, D - 2 * IMG_DEV))[None]


def read_ids(row):
    row = row.astype(jnp.int32)
    return row[:, :IMG_DEV] * ID_BASE + row[:, IMG_DEV : 2 * IMG_DEV]


def weight_messages(core, key_weight, value_weight, pool_query):
    return call(
        weight_kernel, [shape(N_GRP, 24, 128, dtype=bf16)], [pltpu.VMEM((24, 128), f32)],
        in_specs=[SMEM, VMEM, VMEM, VMEM],
    )(core, key_weight, value_weight, pool_query[None])


def context_messages(weights, patches, segments, tail):
    return call(
        context_kernel,
        [shape(HEADS, 16, D, dtype=bf16), shape(D, 128 + HEAD_DIM, dtype=bf16)],
        [
            pltpu.VMEM((D, 128), f32),
            pltpu.VMEM((D, KEY_REST), f32),
            pltpu.VMEM((ROWS // 128, HEADS * 16, 128), f32),
            pltpu.VMEM((HEADS * 16, 128), f32),
        ],
        in_specs=[VMEM] * 4,
    )(weights, patches, segments, tail)


def pooled_messages(near, pair, query):
    return call(
        project_kernel,
        [shape(N_SIDE, N_SIDE, IMG_DEV * HEAD_DIM)],
        [pltpu.VMEM((N_SIDE * 16, 128), f32), pltpu.VMEM((N_SIDE * 16, 128), f32)],
        in_specs=[VMEM] * 3,
    )(near, pair, query)


def unit_messages(side, pooled, tail):
    return call(
        unit_kernel,
        [
            shape(N_FAR, 8, D, dtype=bf16),
            shape(IMG_DEV * N_SIDE, D, dtype=bf16),
            shape(IMG_DEV, D),
            shape(IMG_DEV, 128),
        ],
        [pltpu.VMEM((IMG_DEV, N_SIDE, D), f32), pltpu.VMEM((IMG_DEV, N_SIDE, 128), f32), pltpu.VMEM((8, D), f32)],
        in_specs=[SMEM, VMEM, VMEM],
    )(side, pooled, tail)


def pair_messages(params, side, far, texts, lows, index):
    return call(
        pair_kernel, [shape(N_SIDE, 6 * TILES, 128)], in_specs=[SMEM, SMEM, VMEM, VMEM, VMEM, VMEM]
    )(params, side, far, texts, lows, index)


def gradients(parts, unit_text, text_norm, unit_image, image_norm):
    return call(
        final_kernel,
        [shape(IMG_DEV, D), shape(IMG_DEV, D)],
        [pltpu.VMEM((6 * TILES, 128), f32)],
        in_specs=[VMEM] * 5,
    )(parts, unit_text, text_norm, unit_image, image_norm)


def body(
    patches,
    segment_ids,
    image_ids,
    text_embeds,
    key_weight,
    value_weight,
    pool_query,
    logit_scale,
    logit_bias,
):
    yh, core, yl, x, z = (lax.axis_index(name) for name in FINE)
    side = (core * 2 + yl) * 4 + x
    weights = exchange(weight_messages(core[None], key_weight, value_weight, pool_query), GRP)

    text_full = text_embeds.astype(f32)
    text_norm = jnp.sqrt(jnp.sum(text_full * text_full, axis=1, keepdims=True) + EPS)
    unit_text = text_full / text_norm
    text_low = unit_text.astype(bf16)
    id_row = code_ids(image_ids)
    tail = jnp.concatenate(
        [jnp.zeros((AT_TEXT, D), bf16), text_low, id_row, jnp.zeros((16 - AT_SCALAR, D), bf16)], axis=0
    )
    query = lax.dynamic_slice_in_dim(pool_query, side * HEAD_DIM, HEAD_DIM)[None].astype(f32)
    context, pair = context_messages(weights, patches, segment_ids, tail)
    near = exchange(context, SIDE)
    pooled = exchange(pooled_messages(near, pair, query), SIDE)

    tail = jnp.concatenate(
        [jnp.zeros((IMG_DEV, D), bf16), text_low, id_row, jnp.zeros((1, D), bf16)], axis=0
    )
    far, lows, unit_image, image_norm = unit_messages(side[None], pooled, tail)
    far = exchange(far, FAR)

    texts = jnp.transpose(near[:, AT_TEXT:AT_ID], (1, 0, 2)).reshape(IMG_DEV * N_SIDE, D)
    side_dev = (yh * N_SIDE + jnp.arange(N_SIDE, dtype=jnp.int32)) * 8 + z
    text_index = side_dev[None, :] * IMG_DEV + jnp.arange(IMG_DEV, dtype=jnp.int32)[:, None]
    image_index = read_ids(near[:, AT_ID]).T
    index = jnp.concatenate([text_index, image_index], axis=0).reshape(6 * N_SIDE, 1)
    params = jnp.concatenate([logit_scale, logit_bias])
    parts = exchange(pair_messages(params, side[None], far, texts, lows, index), SIDE)
    return gradients(parts, unit_text, text_norm, unit_image, image_norm)


def solution(mesh):
    fine = Mesh(mesh.devices.reshape(FINE_SHAPE), FINE)
    rows = P(FINE, None)
    in_specs = (rows, rows, P(FINE), rows, P(GRP, None), P(GRP, None), P(), P(), P())
    return jax.shard_map(
        body, mesh=fine, in_specs=in_specs, out_specs=(rows, rows), check_vma=False
    )
```

```python
import math

import jax
import jax.numpy as jnp
from jax import lax
from jax.experimental import pallas as pl
from jax.experimental.pallas import tpu as pltpu
from jax.sharding import Mesh
from jax.sharding import PartitionSpec as P

D = 1152
TILES = D // 128
HEADS = 16
HEAD_DIM = 72
IMG_DEV = 3
PAIRS = 1536
EPS = 1e-06
ID_BASE = 64
ROWS = 768
LOW = -1e30

FINE = ("yh", "core", "yl", "x", "z")
FINE_SHAPE = (4, 2, 2, 4, 8)
SIDE = ("core", "yl", "x")
FAR = ("yh", "z")
GRP = ("yl", "x", "z")
N_SIDE = 16
N_FAR = 32
N_GRP = 64
W_ROWS = 18

AT_FOLDED = HEAD_DIM
AT_KEY = AT_FOLDED + HEADS
KEY_FIRST = 128 - AT_KEY
KEY_REST = HEAD_DIM - KEY_FIRST

TOPS = 2
AT_TOP = IMG_DEV
AT_TEXT = AT_TOP + TOPS * IMG_DEV
AT_ID = AT_TEXT + IMG_DEV
NEAR_LIST = AT_ID + 1
NEAR_ROWS = 120
AT_NEAR_ID = AT_ID
AT_SCALAR = NEAR_LIST + AT_ID
N_LANES = 8

AT_FAR_ID = 6 * TILES
FAR_ROWS = 56

f32 = jnp.float32
bf16 = jnp.bfloat16
VMEM = pl.BlockSpec(memory_space=pltpu.VMEM)
ANY = pl.BlockSpec(memory_space=pltpu.HBM)
SMEM = pl.BlockSpec(memory_space=pltpu.SMEM)


def call(kernel, outs, scratch=(), limit=40, **cost):
    many = len(outs) > 1
    return pl.pallas_call(
        kernel,
        out_shape=tuple(outs) if many else outs[0],
        out_specs=(VMEM,) * len(outs) if many else VMEM,
        scratch_shapes=list(scratch),
        compiler_params=pltpu.CompilerParams(vmem_limit_bytes=limit * 1024 * 1024),
        **cost,
    )


def shape(*dims, dtype=f32):
    return jax.ShapeDtypeStruct(dims, dtype)


def iota(dims, axis):
    return lax.broadcasted_iota(jnp.int32, dims, axis)


def dot_nt(a, b):
    return lax.dot_general(a, b, (((1,), (1,)), ((), ())), preferred_element_type=f32)


def dot(a, b):
    return jnp.dot(a, b, preferred_element_type=f32)


def exchange(blocks, axes):
    return lax.all_to_all(blocks, axes, 0, 0)


def weight_kernel(core_ref, key_hbm, value_hbm, query_hbm, out_ref, key_ref, value_ref, query_ref, tile, sems):
    copies = [
        pltpu.make_async_copy(source, target, sems.at[index])
        for index, (source, target) in enumerate(
            ((query_hbm, query_ref), (key_hbm, key_ref), (value_hbm, value_ref))
        )
    ]
    for copy in copies:
        copy.start()
    members = jnp.where(iota((HEADS, D), 1) // HEAD_DIM == iota((HEADS, D), 0), 1.0, 0.0).astype(bf16)
    tile[...] = jnp.zeros_like(tile)
    for copy in copies:
        copy.wait()
    keys = key_ref[...].astype(f32)
    values = value_ref[...].astype(f32)
    query = query_ref[...].astype(f32)
    query = jnp.concatenate([query[row : row + 1] for row in range(TILES)], axis=1)
    products = keys * query
    high = products.astype(bf16)
    low = (products - high.astype(f32)).astype(bf16)
    folded = (dot_nt(high, members) + dot_nt(low, members)) * (1.0 / math.sqrt(HEAD_DIM))
    mine = core_ref[0] == 0
    half = HEADS // 2 * HEAD_DIM
    keys = jnp.where(mine, keys[:, :half], keys[:, half:])
    values = jnp.where(mine, values[:, :half], values[:, half:])
    for head in range(HEADS // 2):
        at = head * HEAD_DIM
        tile[:W_ROWS, :HEAD_DIM] = values[:, at : at + HEAD_DIM]
        tile[:W_ROWS, AT_FOLDED:AT_KEY] = folded
        tile[:W_ROWS, AT_KEY:] = keys[:, at : at + KEY_FIRST]
        for part in range(3):
            tile[W_ROWS:, part * KEY_REST : (part + 1) * KEY_REST] = keys[
                part * 6 : part * 6 + 6, at + KEY_FIRST : at + HEAD_DIM
            ]
        out_ref[head * 8 : head * 8 + 8] = jnp.broadcast_to(tile[...].astype(bf16)[None], (8, 24, 128))


def three_parts(value):
    first = value.astype(bf16).astype(f32)
    rest = value - first
    second = rest.astype(bf16).astype(f32)
    return first, second, rest - second


def context_kernel(weights_ref, patches_ref, segments_ref, tail_ref, out_ref, main, sums):
    for source in range(N_GRP):
        at = source * W_ROWS
        main[at : at + W_ROWS, :] = weights_ref[source].astype(f32)[:W_ROWS]
    scores = dot(patches_ref[...], main[...].astype(bf16)).T[AT_FOLDED:AT_KEY]

    segments = segments_ref[...]
    masked = jnp.concatenate([jnp.where(segments == slot, scores, LOW) for slot in range(IMG_DEV)], axis=0)
    place = iota((IMG_DEV * HEADS, ROWS), 1)
    peak = jnp.max(masked, axis=1, keepdims=True)
    powers = jnp.where(masked > 0.5 * LOW, jnp.exp(masked - peak), 0.0)
    total = jnp.sum(powers, axis=1, keepdims=True)
    best = peak
    picks, values = [], []
    for top in range(TOPS):
        if top > 0:
            best = jnp.max(masked, axis=1, keepdims=True)
        there = best > 0.5 * LOW
        first = jnp.min(jnp.where(masked == best, place, ROWS), axis=1, keepdims=True)
        hit = (place == first) & there
        picks.append(jnp.where(hit, 1.0, 0.0).astype(bf16))
        masked = jnp.where(hit, LOW, masked)
        powers = jnp.where(hit, 0.0, powers)
        values.append(jnp.where(there, 1.0, 0.0))
    others = powers / total
    context = dot(jnp.concatenate([others.astype(bf16), *picks], axis=0), patches_ref[...])
    values = [
        *three_parts(peak + jnp.log(total)),
        *three_parts(jnp.sum(others, axis=1, keepdims=True)),
        *values,
    ]
    lanes = iota((IMG_DEV * HEADS, 128), 1) - iota((IMG_DEV * HEADS, 128), 0) // HEADS * N_LANES
    scalars = jnp.zeros((IMG_DEV * HEADS, 128), f32)
    for index, value in enumerate(values):
        scalars = jnp.where(lanes == index, value, scalars)
    scalars = scalars[:HEADS] + scalars[HEADS : 2 * HEADS] + scalars[2 * HEADS :]

    def put(row, value):
        sums[pl.ds(row, HEADS, stride=NEAR_ROWS), :] = value

    blank = jnp.zeros((HEADS, 128), f32)
    for tile in range(TILES):
        for row in range(AT_TEXT):
            put(tile * NEAR_LIST + row, context[row * HEADS : (row + 1) * HEADS, tile * 128 : (tile + 1) * 128])
        for row in range(AT_TEXT, NEAR_LIST):
            at = tile * NEAR_LIST + row
            put(at, scalars if at == AT_SCALAR else jnp.broadcast_to(tail_ref[at : at + 1, :], (HEADS, 128)))
    for row in range(TILES * NEAR_LIST, NEAR_ROWS):
        put(row, blank)
    out_ref[...] = sums[...].reshape(HEADS, NEAR_ROWS, 128).astype(bf16)


def project_kernel(place_ref, near_ref, weights_ref, query_ref, out_ref, text_ref, index_ref, rows, main, extra):
    for source in range(N_SIDE):
        rows[source * NEAR_ROWS : (source + 1) * NEAR_ROWS, :] = near_ref[source].astype(f32)
    for source in range(N_GRP):
        block = weights_ref[source].astype(f32)
        at = source * W_ROWS
        main[at : at + W_ROWS, :] = block[:W_ROWS]
        for part in range(3):
            extra[at + part * 6 : at + part * 6 + 6, :] = block[
                W_ROWS:, part * KEY_REST : (part + 1) * KEY_REST
            ]

    def take(row):
        return rows[pl.ds(row, N_SIDE, stride=NEAR_ROWS), :]

    near = jnp.concatenate(
        [
            jnp.concatenate([take(tile * NEAR_LIST + row) for row in range(AT_ID)], axis=0).astype(bf16)
            for tile in range(TILES)
        ],
        axis=1,
    )
    text_ref[...] = near[AT_TEXT * N_SIDE :]
    pair = jnp.concatenate([main[...], main[:, AT_KEY:], extra[...]], axis=1).astype(bf16)
    both = dot(near[: AT_TEXT * N_SIDE], pair)
    count = IMG_DEV * N_SIDE
    scalars = take(AT_SCALAR)
    lanes = iota((N_SIDE, 128), 1)

    def scalar(index):
        return jnp.concatenate(
            [
                jnp.sum(jnp.where(lanes == slot * N_LANES + index, scalars, 0.0), axis=1, keepdims=True)
                for slot in range(IMG_DEV)
            ],
            axis=0,
        )

    level = scalar(0) + scalar(1) + scalar(2)
    others = scalar(3) + scalar(4) + scalar(5)
    some = others > 0.0
    peak = jnp.where(some, 0.0, LOW)
    powers = []
    for top in range(TOPS):
        keys = both[(top + 1) * count : (top + 2) * count, 128:].astype(bf16).astype(f32)
        score = jnp.sum(keys * query_ref[...], axis=1, keepdims=True) / math.sqrt(HEAD_DIM)
        there = scalar(6 + top) > 0.5
        score = jnp.where(there, score - level, LOW)
        peak = jnp.maximum(peak, score)
        powers.append((there, score))
    powers = [jnp.where(there, jnp.exp(score - peak), 0.0) for there, score in powers]
    shift = jnp.where(some, jnp.exp(jnp.where(some, -peak, 0.0)), 0.0)
    total = others * shift
    for power in powers:
        total = total + power
    pooled = both[:count, :HEAD_DIM] * (shift / total)
    for top, power in enumerate(powers):
        value = both[(top + 1) * count : (top + 2) * count, :HEAD_DIM].astype(bf16).astype(f32)
        pooled = pooled + (power / total).astype(bf16).astype(f32) * value
    pooled = jnp.concatenate([pooled[slot * N_SIDE : (slot + 1) * N_SIDE] for slot in range(IMG_DEV)], axis=1)
    out_ref[...] = jnp.broadcast_to(pooled[None], out_ref.shape)

    ids = take(AT_NEAR_ID)
    member = iota((N_SIDE, 1), 0)
    for slot in range(IMG_DEV):
        text = ((place_ref[0] * N_SIDE + member) * 8 + place_ref[1]) * IMG_DEV + slot
        code = jnp.where(lanes == slot, float(ID_BASE), 0.0) + jnp.where(lanes == slot + IMG_DEV, 1.0, 0.0)
        image = jnp.sum(ids * code, axis=1, keepdims=True).astype(jnp.int32)
        index_ref[slot * N_SIDE : (slot + 1) * N_SIDE, :] = text
        index_ref[count + slot * N_SIDE : count + (slot + 1) * N_SIDE, :] = image


def unit_kernel(place_ref, pooled_ref, tail_ref, out_ref, low_ref, unit_ref, norm_ref, units, norms, block):
    side = place_ref[2]
    for slot in range(IMG_DEV):
        for head in range(HEADS):
            units[slot, :, head * HEAD_DIM : (head + 1) * HEAD_DIM] = pooled_ref[
                head, :, slot * HEAD_DIM : (slot + 1) * HEAD_DIM
            ]
    block[...] = tail_ref[...]

    def put(row, value):
        for tile in range(TILES):
            block[tile * 6 + row : tile * 6 + row + 1, :] = value[:, tile * 128 : (tile + 1) * 128]

    for slot in range(IMG_DEV):
        pooled = units[slot]
        norm = jnp.sqrt(jnp.sum(pooled * pooled, axis=1, keepdims=True) + EPS)
        unit = pooled / norm
        units[slot] = unit
        norms[slot] = jnp.broadcast_to(norm, (N_SIDE, 128))
        low_ref[slot * N_SIDE : (slot + 1) * N_SIDE, :] = unit.astype(bf16)
        own = units[slot, pl.ds(side, 1), :]
        put(slot, own)
        unit_ref[slot : slot + 1, :] = own
        norm_ref[slot : slot + 1, :] = norms[slot, pl.ds(side, 1), :]
    out_ref[...] = jnp.broadcast_to(block[...].astype(bf16)[None], out_ref.shape)


def pair_kernel(params_ref, place_ref, far_ref, text_ref, low_ref, index_ref, out_ref, far_rows, sums):
    scale, offset = params_ref[0], params_ref[1]
    for source in range(N_FAR):
        far_rows[source * FAR_ROWS : (source + 1) * FAR_ROWS, :] = far_ref[source].astype(f32)

    def take(row):
        return far_rows[pl.ds(row, N_FAR, stride=FAR_ROWS), :].astype(bf16)

    digit = iota((8, 128), 1)
    slot = iota((8, 128), 0)
    code = jnp.where(digit == slot, float(ID_BASE), 0.0) + jnp.where(digit == slot + IMG_DEV, 1.0, 0.0)
    ids = dot_nt(jnp.where(slot < IMG_DEV, code, 0.0).astype(bf16), take(AT_FAR_ID))
    ids = jnp.concatenate([ids[row : row + 1] for row in range(IMG_DEV)], axis=1).astype(jnp.int32)
    columns = IMG_DEV * N_FAR
    column = iota((1, columns), 1)
    device = column % N_FAR
    device = ((device // 8) * N_SIDE + place_ref[2]) * 8 + device % 8
    text_index = device * IMG_DEV + column // N_FAR
    sums[...] = jnp.zeros_like(sums)
    for first, near, index, place in ((0, text_ref[...], ids, 0), (IMG_DEV, low_ref[...], text_index, 1)):
        far = jnp.concatenate(
            [
                jnp.concatenate([take(tile * 6 + first + row) for row in range(IMG_DEV)], axis=0)
                for tile in range(TILES)
            ],
            axis=1,
        )
        logits = scale * dot_nt(near, far) + offset
        own = index_ref[place * IMG_DEV * N_SIDE : (place + 1) * IMG_DEV * N_SIDE, :]
        pair_sign = jnp.where(own == index, 1.0, -1.0)
        scaled = scale * (-pair_sign * jax.nn.sigmoid(-pair_sign * logits) / PAIRS)
        parts = dot(scaled.astype(bf16), far)
        for tile in range(TILES):
            for row in range(IMG_DEV):
                sums[pl.ds(tile * 6 + first + row, N_SIDE, stride=FAR_ROWS), :] = parts[
                    row * N_SIDE : (row + 1) * N_SIDE, tile * 128 : (tile + 1) * 128
                ]
    out_ref[...] = sums[...].reshape(N_SIDE, FAR_ROWS, 128).astype(bf16)


def final_kernel(parts_ref, unit_text_ref, text_norm_ref, unit_image_ref, image_norm_ref, image_ref, text_ref, sums):
    total = parts_ref[0].astype(f32)
    for source in range(1, N_SIDE):
        total = total + parts_ref[source].astype(f32)
    sums[...] = total
    whole = jnp.concatenate([sums[tile * 6 : tile * 6 + 6, :] for tile in range(TILES)], axis=1)
    for first, unit_ref, norm, out_ref in (
        (0, unit_text_ref, text_norm_ref[:, :1], text_ref),
        (IMG_DEV, unit_image_ref, image_norm_ref[:, :1], image_ref),
    ):
        part = whole[first : first + IMG_DEV]
        unit = unit_ref[...]
        out_ref[...] = (part - unit * jnp.sum(unit * part, axis=1, keepdims=True)) / norm


def tiled_rows(array):
    rows = array.shape[0]
    return jnp.transpose(array.reshape(rows, TILES, 128), (1, 0, 2))


def code_ids(ids):
    row = jnp.concatenate([ids // ID_BASE, ids % ID_BASE]).astype(f32)
    return jnp.pad(row, (0, 128 - 2 * IMG_DEV))[None]


def weight_messages(core, key_weight, value_weight, pool_query):
    return call(
        weight_kernel,
        [shape(N_GRP, 24, 128, dtype=bf16)],
        [
            pltpu.VMEM((W_ROWS, D), bf16),
            pltpu.VMEM((W_ROWS, D), bf16),
            pltpu.VMEM((TILES, 128), bf16),
            pltpu.VMEM((24, 128), f32),
            pltpu.SemaphoreType.DMA((3,)),
        ],
        limit=62,
        in_specs=[SMEM, ANY, ANY, ANY],
    )(core, key_weight, value_weight, pool_query.reshape(TILES, 128))


def fetch_kernel(patches_hbm, segments_hbm, patches_ref, segments_ref, sems):
    copies = [
        pltpu.make_async_copy(patches_hbm, patches_ref, sems.at[0]),
        pltpu.make_async_copy(segments_hbm, segments_ref, sems.at[1]),
    ]
    for copy in copies:
        copy.start()
    for copy in copies:
        copy.wait()


def fetch(patches, segments):
    return call(
        fetch_kernel,
        [shape(ROWS, D, dtype=bf16), shape(1, ROWS, dtype=jnp.int32)],
        [pltpu.SemaphoreType.DMA((2,))],
        in_specs=[ANY, ANY],
    )(patches, segments)


def context_messages(weights, patches, segments, tail):
    return call(
        context_kernel,
        [shape(HEADS, NEAR_ROWS, 128, dtype=bf16)],
        [pltpu.VMEM((D, 128), f32), pltpu.VMEM((HEADS * NEAR_ROWS, 128), f32)],
        in_specs=[VMEM] * 4,
    )(weights, patches, segments, tail)


def pooled_messages(place, near, weights, query):
    return call(
        project_kernel,
        [
            shape(N_SIDE, N_SIDE, IMG_DEV * HEAD_DIM),
            shape(IMG_DEV * N_SIDE, D, dtype=bf16),
            shape(2 * IMG_DEV * N_SIDE, 1, dtype=jnp.int32),
        ],
        [
            pltpu.VMEM((N_SIDE * NEAR_ROWS, 128), f32),
            pltpu.VMEM((D, 128), f32),
            pltpu.VMEM((D, KEY_REST), f32),
        ],
        in_specs=[SMEM] + [VMEM] * 3,
    )(place, near, weights, query)


def unit_messages(place, pooled, tail):
    return call(
        unit_kernel,
        [
            shape(N_FAR, FAR_ROWS, 128, dtype=bf16),
            shape(IMG_DEV * N_SIDE, D, dtype=bf16),
            shape(IMG_DEV, D),
            shape(IMG_DEV, 128),
        ],
        [pltpu.VMEM((IMG_DEV, N_SIDE, D), f32), pltpu.VMEM((IMG_DEV, N_SIDE, 128), f32), pltpu.VMEM((FAR_ROWS, 128), f32)],
        in_specs=[SMEM, VMEM, VMEM],
    )(place, pooled, tail)


def pair_messages(params, place, far, texts, lows, index):
    return call(
        pair_kernel,
        [shape(N_SIDE, FAR_ROWS, 128, dtype=bf16)],
        [pltpu.VMEM((N_FAR * FAR_ROWS, 128), f32), pltpu.VMEM((N_SIDE * FAR_ROWS, 128), f32)],
        in_specs=[SMEM, SMEM, VMEM, VMEM, VMEM, VMEM],
    )(params, place, far, texts, lows, index)


def gradients(parts, unit_text, text_norm, unit_image, image_norm):
    return call(
        final_kernel,
        [shape(IMG_DEV, D), shape(IMG_DEV, D)],
        [pltpu.VMEM((FAR_ROWS, 128), f32)],
        in_specs=[VMEM] * 5,
    )(parts, unit_text, text_norm, unit_image, image_norm)


def body(
    patches,
    segment_ids,
    image_ids,
    text_embeds,
    key_weight,
    value_weight,
    pool_query,
    logit_scale,
    logit_bias,
):
    yh, core, yl, x, z = (lax.axis_index(name) for name in FINE)
    side = (core * 2 + yl) * 4 + x
    weights = exchange(weight_messages(core[None], key_weight, value_weight, pool_query), GRP)

    text_full = text_embeds.astype(f32)
    text_norm = jnp.sqrt(jnp.sum(text_full * text_full, axis=1, keepdims=True) + EPS)
    unit_text = text_full / text_norm
    text_norm = jnp.broadcast_to(text_norm, (IMG_DEV, 128))
    text_low = tiled_rows(lax.reduce_precision(unit_text, 8, 7))
    ids = code_ids(image_ids)
    near_tail = jnp.pad(text_low, ((0, 0), (AT_TEXT, 1), (0, 0))).reshape(TILES * NEAR_LIST, 128)
    near_tail = jnp.where(jnp.arange(TILES * NEAR_LIST)[:, None] == AT_NEAR_ID, ids, near_tail)
    far_tail = jnp.pad(text_low, ((0, 0), (IMG_DEV, 0), (0, 0))).reshape(6 * TILES, 128)
    far_tail = jnp.concatenate([far_tail, ids, jnp.zeros((1, 128), f32)], axis=0)
    query = lax.dynamic_slice_in_dim(pool_query, side * HEAD_DIM, HEAD_DIM)[None].astype(f32)
    patches, segments = fetch(patches, segment_ids)
    params = jnp.concatenate([logit_scale, logit_bias])
    place = jnp.stack([yh, z, side])
    (weights, patches, segments, near_tail, far_tail, query, params, place, unit_text, text_norm) = (
        lax.optimization_barrier(
            (weights, patches, segments, near_tail, far_tail, query, params, place, unit_text, text_norm)
        )
    )

    near = exchange(context_messages(weights, patches, segments, near_tail), SIDE)
    pooled, texts, index = pooled_messages(place, near, weights, query)
    pooled = exchange(pooled, SIDE)
    far, lows, unit_image, image_norm = unit_messages(place, pooled, far_tail)
    far = exchange(far, FAR)
    parts = exchange(pair_messages(params, place, far, texts, lows, index), SIDE)
    return gradients(parts, unit_text, text_norm, unit_image, image_norm)


def solution(mesh):
    fine = Mesh(mesh.devices.reshape(FINE_SHAPE), FINE)
    rows = P(FINE, None)
    in_specs = (rows, rows, P(FINE), rows, P(GRP, None), P(GRP, None), P(), P(), P())
    return jax.shard_map(
        body, mesh=fine, in_specs=in_specs, out_specs=(rows, rows), check_vma=False
    )
```

```python
import math

import jax
import jax.numpy as jnp
from jax import lax
from jax.experimental import pallas as pl
from jax.experimental.pallas import tpu as pltpu
from jax.sharding import Mesh
from jax.sharding import PartitionSpec as P

D = 1152
TILES = D // 128
HEADS = 16
HEAD_DIM = 72
IMG_DEV = 3
PAIRS = 1536
EPS = 1e-06
ID_BASE = 64
ROWS = 768
LOW = -1e30

FINE = ("yh", "core", "yl", "x", "z")
FINE_SHAPE = (4, 2, 2, 4, 8)
SIDE = ("core", "yl", "x")
FAR = ("yh", "z")
GRP = ("yl", "x", "z")
N_SIDE = 16
N_FAR = 32
N_GRP = 64
W_ROWS = 18

AT_FOLDED = HEAD_DIM
AT_KEY = AT_FOLDED + HEADS
KEY_FIRST = 128 - AT_KEY
KEY_REST = HEAD_DIM - KEY_FIRST

TOPS = 2
AT_TOP = IMG_DEV
AT_TEXT = AT_TOP + TOPS * IMG_DEV
AT_ID = AT_TEXT + IMG_DEV
NEAR_LIST = AT_ID + 1
NEAR_ROWS = 120
AT_NEAR_ID = AT_ID
AT_SCALAR = NEAR_LIST + AT_ID
N_LANES = 8

AT_FAR_ID = 6 * TILES
FAR_ROWS = 56

f32 = jnp.float32
bf16 = jnp.bfloat16
VMEM = pl.BlockSpec(memory_space=pltpu.VMEM)
ANY = pl.BlockSpec(memory_space=pltpu.HBM)
SMEM = pl.BlockSpec(memory_space=pltpu.SMEM)


def call(kernel, outs, scratch=(), limit=40, **cost):
    many = len(outs) > 1
    return pl.pallas_call(
        kernel,
        out_shape=tuple(outs) if many else outs[0],
        out_specs=(VMEM,) * len(outs) if many else VMEM,
        scratch_shapes=list(scratch),
        compiler_params=pltpu.CompilerParams(vmem_limit_bytes=limit * 1024 * 1024),
        **cost,
    )


def shape(*dims, dtype=f32):
    return jax.ShapeDtypeStruct(dims, dtype)


def iota(dims, axis):
    return lax.broadcasted_iota(jnp.int32, dims, axis)


def dot_nt(a, b):
    return lax.dot_general(a, b, (((1,), (1,)), ((), ())), preferred_element_type=f32)


def dot(a, b):
    return jnp.dot(a, b, preferred_element_type=f32)


def exchange(blocks, axes):
    return lax.all_to_all(blocks, axes, 0, 0)


def weight_kernel(core_ref, key_hbm, value_hbm, query_hbm, out_ref, key_ref, value_ref, query_ref, tile, sems):
    copies = [
        pltpu.make_async_copy(source, target, sems.at[index])
        for index, (source, target) in enumerate(
            ((query_hbm, query_ref), (key_hbm, key_ref), (value_hbm, value_ref))
        )
    ]
    for copy in copies:
        copy.start()
    members = jnp.where(iota((HEADS, D), 1) // HEAD_DIM == iota((HEADS, D), 0), 1.0, 0.0).astype(bf16)
    tile[...] = jnp.zeros_like(tile)
    for copy in copies:
        copy.wait()
    keys = key_ref[...].astype(f32)
    values = value_ref[...].astype(f32)
    query = query_ref[...].astype(f32)
    query = jnp.concatenate([query[row : row + 1] for row in range(TILES)], axis=1)
    products = keys * query
    high = products.astype(bf16)
    low = (products - high.astype(f32)).astype(bf16)
    folded = (dot_nt(high, members) + dot_nt(low, members)) * (1.0 / math.sqrt(HEAD_DIM))
    mine = core_ref[0] == 0
    half = HEADS // 2 * HEAD_DIM
    keys = jnp.where(mine, keys[:, :half], keys[:, half:])
    values = jnp.where(mine, values[:, :half], values[:, half:])
    for head in range(HEADS // 2):
        at = head * HEAD_DIM
        tile[:W_ROWS, :HEAD_DIM] = values[:, at : at + HEAD_DIM]
        tile[:W_ROWS, AT_FOLDED:AT_KEY] = folded
        tile[:W_ROWS, AT_KEY:] = keys[:, at : at + KEY_FIRST]
        for part in range(3):
            tile[W_ROWS:, part * KEY_REST : (part + 1) * KEY_REST] = keys[
                part * 6 : part * 6 + 6, at + KEY_FIRST : at + HEAD_DIM
            ]
        out_ref[head * 8 : head * 8 + 8] = jnp.broadcast_to(tile[...].astype(bf16)[None], (8, 24, 128))


def three_parts(value):
    first = value.astype(bf16).astype(f32)
    rest = value - first
    second = rest.astype(bf16).astype(f32)
    return first, second, rest - second


def context_kernel(weights_ref, patches_ref, segments_ref, tail_ref, out_ref, main, sums):
    for source in range(N_GRP):
        at = source * W_ROWS
        main[at : at + W_ROWS, :] = weights_ref[source].astype(f32)[:W_ROWS]
    scores = dot(patches_ref[...], main[...].astype(bf16)).T[AT_FOLDED:AT_KEY]

    segments = segments_ref[...]
    masked = jnp.concatenate([jnp.where(segments == slot, scores, LOW) for slot in range(IMG_DEV)], axis=0)
    place = iota((IMG_DEV * HEADS, ROWS), 1)
    peak = jnp.max(masked, axis=1, keepdims=True)
    powers = jnp.where(masked > 0.5 * LOW, jnp.exp(masked - peak), 0.0)
    total = jnp.sum(powers, axis=1, keepdims=True)
    best = peak
    picks, values = [], []
    for top in range(TOPS):
        if top > 0:
            best = jnp.max(masked, axis=1, keepdims=True)
        there = best > 0.5 * LOW
        first = jnp.min(jnp.where(masked == best, place, ROWS), axis=1, keepdims=True)
        hit = (place == first) & there
        picks.append(jnp.where(hit, 1.0, 0.0).astype(bf16))
        masked = jnp.where(hit, LOW, masked)
        powers = jnp.where(hit, 0.0, powers)
        values.append(jnp.where(there, 1.0, 0.0))
    others = powers / total
    context = dot(jnp.concatenate([others.astype(bf16), *picks], axis=0), patches_ref[...])
    values = [
        *three_parts(peak + jnp.log(total)),
        *three_parts(jnp.sum(others, axis=1, keepdims=True)),
        *values,
    ]
    lanes = iota((IMG_DEV * HEADS, 128), 1) - iota((IMG_DEV * HEADS, 128), 0) // HEADS * N_LANES
    scalars = jnp.zeros((IMG_DEV * HEADS, 128), f32)
    for index, value in enumerate(values):
        scalars = jnp.where(lanes == index, value, scalars)
    scalars = scalars[:HEADS] + scalars[HEADS : 2 * HEADS] + scalars[2 * HEADS :]

    def put(row, value):
        sums[pl.ds(row, HEADS, stride=NEAR_ROWS), :] = value

    blank = jnp.zeros((HEADS, 128), f32)
    for tile in range(TILES):
        for row in range(AT_TEXT):
            put(tile * NEAR_LIST + row, context[row * HEADS : (row + 1) * HEADS, tile * 128 : (tile + 1) * 128])
        for row in range(AT_TEXT, NEAR_LIST):
            at = tile * NEAR_LIST + row
            put(at, scalars if at == AT_SCALAR else jnp.broadcast_to(tail_ref[at : at + 1, :], (HEADS, 128)))
    for row in range(TILES * NEAR_LIST, NEAR_ROWS):
        put(row, blank)
    out_ref[...] = sums[...].reshape(HEADS, NEAR_ROWS, 128).astype(bf16)


def project_kernel(place_ref, near_ref, weights_ref, query_ref, out_ref, text_ref, index_ref, rows, main, extra):
    for source in range(N_SIDE):
        rows[source * NEAR_ROWS : (source + 1) * NEAR_ROWS, :] = near_ref[source].astype(f32)
    for source in range(N_GRP):
        block = weights_ref[source].astype(f32)
        at = source * W_ROWS
        main[at : at + W_ROWS, :] = block[:W_ROWS]
        for part in range(3):
            extra[at + part * 6 : at + part * 6 + 6, :] = block[
                W_ROWS:, part * KEY_REST : (part + 1) * KEY_REST
            ]

    def take(row):
        return rows[pl.ds(row, N_SIDE, stride=NEAR_ROWS), :]

    near = jnp.concatenate(
        [
            jnp.concatenate([take(tile * NEAR_LIST + row) for row in range(AT_ID)], axis=0).astype(bf16)
            for tile in range(TILES)
        ],
        axis=1,
    )
    text_ref[...] = near[AT_TEXT * N_SIDE :]
    pair = jnp.concatenate([main[...], main[:, AT_KEY:], extra[...]], axis=1).astype(bf16)
    both = dot(near[: AT_TEXT * N_SIDE], pair)
    count = IMG_DEV * N_SIDE
    scalars = take(AT_SCALAR)
    lanes = iota((N_SIDE, 128), 1)

    def scalar(index):
        return jnp.concatenate(
            [
                jnp.sum(jnp.where(lanes == slot * N_LANES + index, scalars, 0.0), axis=1, keepdims=True)
                for slot in range(IMG_DEV)
            ],
            axis=0,
        )

    level = scalar(0) + scalar(1) + scalar(2)
    others = scalar(3) + scalar(4) + scalar(5)
    some = others > 0.0
    peak = jnp.where(some, 0.0, LOW)
    powers = []
    for top in range(TOPS):
        keys = both[(top + 1) * count : (top + 2) * count, 128:].astype(bf16).astype(f32)
        score = jnp.sum(keys * query_ref[...], axis=1, keepdims=True) / math.sqrt(HEAD_DIM)
        there = scalar(6 + top) > 0.5
        score = jnp.where(there, score - level, LOW)
        peak = jnp.maximum(peak, score)
        powers.append((there, score))
    powers = [jnp.where(there, jnp.exp(score - peak), 0.0) for there, score in powers]
    shift = jnp.where(some, jnp.exp(jnp.where(some, -peak, 0.0)), 0.0)
    total = others * shift
    for power in powers:
        total = total + power
    pooled = both[:count, :HEAD_DIM] * (shift / total)
    for top, power in enumerate(powers):
        value = both[(top + 1) * count : (top + 2) * count, :HEAD_DIM].astype(bf16).astype(f32)
        pooled = pooled + (power / total).astype(bf16).astype(f32) * value
    pooled = jnp.concatenate([pooled[slot * N_SIDE : (slot + 1) * N_SIDE] for slot in range(IMG_DEV)], axis=1)
    out_ref[...] = jnp.broadcast_to(pooled[None], out_ref.shape)

    ids = take(AT_NEAR_ID)
    member = iota((N_SIDE, 1), 0)
    for slot in range(IMG_DEV):
        text = ((place_ref[0] * N_SIDE + member) * 8 + place_ref[1]) * IMG_DEV + slot
        code = jnp.where(lanes == slot, float(ID_BASE), 0.0) + jnp.where(lanes == slot + IMG_DEV, 1.0, 0.0)
        image = jnp.sum(ids * code, axis=1, keepdims=True).astype(jnp.int32)
        index_ref[slot * N_SIDE : (slot + 1) * N_SIDE, :] = text
        index_ref[count + slot * N_SIDE : count + (slot + 1) * N_SIDE, :] = image


def unit_kernel(place_ref, pooled_ref, tail_ref, out_ref, low_ref, unit_ref, norm_ref, units, norms, block):
    side = place_ref[2]
    for slot in range(IMG_DEV):
        for head in range(HEADS):
            units[slot, :, head * HEAD_DIM : (head + 1) * HEAD_DIM] = pooled_ref[
                head, :, slot * HEAD_DIM : (slot + 1) * HEAD_DIM
            ]
    block[...] = tail_ref[...]

    def put(row, value):
        for tile in range(TILES):
            block[tile * 6 + row : tile * 6 + row + 1, :] = value[:, tile * 128 : (tile + 1) * 128]

    for slot in range(IMG_DEV):
        pooled = units[slot]
        norm = jnp.sqrt(jnp.sum(pooled * pooled, axis=1, keepdims=True) + EPS)
        unit = pooled / norm
        units[slot] = unit
        norms[slot] = jnp.broadcast_to(norm, (N_SIDE, 128))
        low_ref[slot * N_SIDE : (slot + 1) * N_SIDE, :] = unit.astype(bf16)
        own = units[slot, pl.ds(side, 1), :]
        put(slot, own)
        unit_ref[slot : slot + 1, :] = own
        norm_ref[slot : slot + 1, :] = norms[slot, pl.ds(side, 1), :]
    out_ref[...] = jnp.broadcast_to(block[...].astype(bf16)[None], out_ref.shape)


def pair_kernel(params_ref, place_ref, far_ref, text_ref, low_ref, index_ref, out_ref, far_rows, sums):
    scale, offset = params_ref[0], params_ref[1]
    for source in range(N_FAR):
        far_rows[source * FAR_ROWS : (source + 1) * FAR_ROWS, :] = far_ref[source].astype(f32)

    def take(row):
        return far_rows[pl.ds(row, N_FAR, stride=FAR_ROWS), :].astype(bf16)

    digit = iota((8, 128), 1)
    slot = iota((8, 128), 0)
    code = jnp.where(digit == slot, float(ID_BASE), 0.0) + jnp.where(digit == slot + IMG_DEV, 1.0, 0.0)
    ids = dot_nt(jnp.where(slot < IMG_DEV, code, 0.0).astype(bf16), take(AT_FAR_ID))
    ids = jnp.concatenate([ids[row : row + 1] for row in range(IMG_DEV)], axis=1).astype(jnp.int32)
    columns = IMG_DEV * N_FAR
    column = iota((1, columns), 1)
    device = column % N_FAR
    device = ((device // 8) * N_SIDE + place_ref[2]) * 8 + device % 8
    text_index = device * IMG_DEV + column // N_FAR
    sums[...] = jnp.zeros_like(sums)
    for first, near, index, place in ((0, text_ref[...], ids, 0), (IMG_DEV, low_ref[...], text_index, 1)):
        far = jnp.concatenate(
            [
                jnp.concatenate([take(tile * 6 + first + row) for row in range(IMG_DEV)], axis=0)
                for tile in range(TILES)
            ],
            axis=1,
        )
        logits = scale * dot_nt(near, far) + offset
        own = index_ref[place * IMG_DEV * N_SIDE : (place + 1) * IMG_DEV * N_SIDE, :]
        pair_sign = jnp.where(own == index, 1.0, -1.0)
        scaled = scale * (-pair_sign * jax.nn.sigmoid(-pair_sign * logits) / PAIRS)
        parts = dot(scaled.astype(bf16), far)
        for tile in range(TILES):
            for row in range(IMG_DEV):
                sums[pl.ds(tile * 6 + first + row, N_SIDE, stride=FAR_ROWS), :] = parts[
                    row * N_SIDE : (row + 1) * N_SIDE, tile * 128 : (tile + 1) * 128
                ]
    out_ref[...] = sums[...].reshape(N_SIDE, FAR_ROWS, 128).astype(bf16)


def final_kernel(parts_ref, unit_text_ref, text_norm_ref, unit_image_ref, image_norm_ref, image_ref, text_ref, sums):
    total = parts_ref[0].astype(f32)
    for source in range(1, N_SIDE):
        total = total + parts_ref[source].astype(f32)
    sums[...] = total
    whole = jnp.concatenate([sums[tile * 6 : tile * 6 + 6, :] for tile in range(TILES)], axis=1)
    for first, unit_ref, norm, out_ref in (
        (0, unit_text_ref, text_norm_ref[:, :1], text_ref),
        (IMG_DEV, unit_image_ref, image_norm_ref[:, :1], image_ref),
    ):
        part = whole[first : first + IMG_DEV]
        unit = unit_ref[...]
        out_ref[...] = (part - unit * jnp.sum(unit * part, axis=1, keepdims=True)) / norm


def tiled_rows(array):
    rows = array.shape[0]
    return jnp.transpose(array.reshape(rows, TILES, 128), (1, 0, 2))


def code_ids(ids):
    row = jnp.concatenate([ids // ID_BASE, ids % ID_BASE]).astype(f32)
    return jnp.pad(row, (0, 128 - 2 * IMG_DEV))[None]


def weight_messages(core, key_weight, value_weight, pool_query):
    return call(
        weight_kernel,
        [shape(N_GRP, 24, 128, dtype=bf16)],
        [
            pltpu.VMEM((W_ROWS, D), bf16),
            pltpu.VMEM((W_ROWS, D), bf16),
            pltpu.VMEM((TILES, 128), bf16),
            pltpu.VMEM((24, 128), f32),
            pltpu.SemaphoreType.DMA((3,)),
        ],
        limit=62,
        in_specs=[SMEM, ANY, ANY, ANY],
    )(core, key_weight, value_weight, pool_query.reshape(TILES, 128))


def fetch_kernel(patches_hbm, segments_hbm, patches_ref, segments_ref, sems):
    copies = [
        pltpu.make_async_copy(patches_hbm, patches_ref, sems.at[0]),
        pltpu.make_async_copy(segments_hbm, segments_ref, sems.at[1]),
    ]
    for copy in copies:
        copy.start()
    for copy in copies:
        copy.wait()


def fetch(patches, segments):
    return call(
        fetch_kernel,
        [shape(ROWS, D, dtype=bf16), shape(1, ROWS, dtype=jnp.int32)],
        [pltpu.SemaphoreType.DMA((2,))],
        in_specs=[ANY, ANY],
    )(patches, segments)


def context_messages(weights, patches, segments, tail):
    return call(
        context_kernel,
        [shape(HEADS, NEAR_ROWS, 128, dtype=bf16)],
        [pltpu.VMEM((D, 128), f32), pltpu.VMEM((HEADS * NEAR_ROWS, 128), f32)],
        in_specs=[VMEM] * 4,
    )(weights, patches, segments, tail)


def pooled_messages(place, near, weights, query):
    return call(
        project_kernel,
        [
            shape(N_SIDE, N_SIDE, IMG_DEV * HEAD_DIM),
            shape(IMG_DEV * N_SIDE, D, dtype=bf16),
            shape(2 * IMG_DEV * N_SIDE, 1, dtype=jnp.int32),
        ],
        [
            pltpu.VMEM((N_SIDE * NEAR_ROWS, 128), f32),
            pltpu.VMEM((D, 128), f32),
            pltpu.VMEM((D, KEY_REST), f32),
        ],
        in_specs=[SMEM] + [VMEM] * 3,
    )(place, near, weights, query)


def unit_messages(place, pooled, tail):
    return call(
        unit_kernel,
        [
            shape(N_FAR, FAR_ROWS, 128, dtype=bf16),
            shape(IMG_DEV * N_SIDE, D, dtype=bf16),
            shape(IMG_DEV, D),
            shape(IMG_DEV, 128),
        ],
        [pltpu.VMEM((IMG_DEV, N_SIDE, D), f32), pltpu.VMEM((IMG_DEV, N_SIDE, 128), f32), pltpu.VMEM((FAR_ROWS, 128), f32)],
        in_specs=[SMEM, VMEM, VMEM],
    )(place, pooled, tail)


def pair_messages(params, place, far, texts, lows, index):
    return call(
        pair_kernel,
        [shape(N_SIDE, FAR_ROWS, 128, dtype=bf16)],
        [pltpu.VMEM((N_FAR * FAR_ROWS, 128), f32), pltpu.VMEM((N_SIDE * FAR_ROWS, 128), f32)],
        in_specs=[SMEM, SMEM, VMEM, VMEM, VMEM, VMEM],
    )(params, place, far, texts, lows, index)


def gradients(parts, unit_text, text_norm, unit_image, image_norm):
    return call(
        final_kernel,
        [shape(IMG_DEV, D), shape(IMG_DEV, D)],
        [pltpu.VMEM((FAR_ROWS, 128), f32)],
        in_specs=[VMEM] * 5,
    )(parts, unit_text, text_norm, unit_image, image_norm)


def body(
    patches,
    segment_ids,
    image_ids,
    text_embeds,
    key_weight,
    value_weight,
    pool_query,
    logit_scale,
    logit_bias,
):
    yh, core, yl, x, z = (lax.axis_index(name) for name in FINE)
    side = (core * 2 + yl) * 4 + x
    weights = exchange(weight_messages(core[None], key_weight, value_weight, pool_query), GRP)

    text_full = text_embeds.astype(f32)
    text_norm = jnp.sqrt(jnp.sum(text_full * text_full, axis=1, keepdims=True) + EPS)
    unit_text = text_full / text_norm
    text_norm = jnp.broadcast_to(text_norm, (IMG_DEV, 128))
    text_low = tiled_rows(lax.reduce_precision(unit_text, 8, 7))
    ids = code_ids(image_ids)
    near_tail = jnp.pad(text_low, ((0, 0), (AT_TEXT, 1), (0, 0))).reshape(TILES * NEAR_LIST, 128)
    near_tail = jnp.where(jnp.arange(TILES * NEAR_LIST)[:, None] == AT_NEAR_ID, ids, near_tail)
    far_tail = jnp.pad(text_low, ((0, 0), (IMG_DEV, 0), (0, 0))).reshape(6 * TILES, 128)
    far_tail = jnp.concatenate([far_tail, ids, jnp.zeros((1, 128), f32)], axis=0)
    query = lax.dynamic_slice_in_dim(pool_query, side * HEAD_DIM, HEAD_DIM)[None].astype(f32)
    patches, segments = fetch(patches, segment_ids)
    params = jnp.concatenate([logit_scale, logit_bias])
    place = jnp.stack([yh, z, side])
    weights, near_tail, far_tail, query, params, place, unit_text, text_norm = lax.optimization_barrier(
        (weights, near_tail, far_tail, query, params, place, unit_text, text_norm)
    )

    near = exchange(context_messages(weights, patches, segments, near_tail), SIDE)
    pooled, texts, index = pooled_messages(place, near, weights, query)
    pooled = exchange(pooled, SIDE)
    far, lows, unit_image, image_norm = unit_messages(place, pooled, far_tail)
    far = exchange(far, FAR)
    parts = exchange(pair_messages(params, place, far, texts, lows, index), SIDE)
    return gradients(parts, unit_text, text_norm, unit_image, image_norm)


def solution(mesh):
    fine = Mesh(mesh.devices.reshape(FINE_SHAPE), FINE)
    rows = P(FINE, None)
    in_specs = (rows, rows, P(FINE), rows, P(GRP, None), P(GRP, None), P(), P(), P())
    return jax.shard_map(
        body, mesh=fine, in_specs=in_specs, out_specs=(rows, rows), check_vma=False
    )
```

```python
import math

import jax
import jax.numpy as jnp
from jax import lax
from jax.experimental import pallas as pl
from jax.experimental.pallas import tpu as pltpu
from jax.sharding import Mesh
from jax.sharding import PartitionSpec as P

D = 1152
TILES = D // 128
HEADS = 16
HEAD_DIM = 72
IMG_DEV = 3
PAIRS = 1536
EPS = 1e-06
ID_BASE = 64
ROWS = 768
CHUNKS = 3
LOW = -1e30

FINE = ("yh", "core", "yl", "x", "z")
FINE_SHAPE = (4, 2, 2, 4, 8)
SIDE = ("core", "yl", "x")
FAR = ("yh", "z")
GRP = ("yl", "x", "z")
N_SIDE = 16
N_FAR = 32
N_GRP = 64
W_ROWS = 18

AT_FOLDED = HEAD_DIM
AT_KEY = AT_FOLDED + HEADS
KEY_FIRST = 128 - AT_KEY
KEY_REST = HEAD_DIM - KEY_FIRST

TOPS = 2
AT_TOP = IMG_DEV
AT_TEXT = AT_TOP + TOPS * IMG_DEV
AT_ID = AT_TEXT + IMG_DEV
NEAR_LIST = AT_ID + 1
NEAR_ROWS = 120
AT_NEAR_ID = AT_ID
AT_SCALAR = NEAR_LIST + AT_ID
N_LANES = 8

AT_FAR_ID = 6 * TILES
FAR_ROWS = 56

f32 = jnp.float32
bf16 = jnp.bfloat16
VMEM = pl.BlockSpec(memory_space=pltpu.VMEM)
ANY = pl.BlockSpec(memory_space=pltpu.HBM)
SMEM = pl.BlockSpec(memory_space=pltpu.SMEM)


def call(kernel, outs, scratch=(), limit=40, **cost):
    many = len(outs) > 1
    return pl.pallas_call(
        kernel,
        out_shape=tuple(outs) if many else outs[0],
        out_specs=(VMEM,) * len(outs) if many else VMEM,
        scratch_shapes=list(scratch),
        compiler_params=pltpu.CompilerParams(vmem_limit_bytes=limit * 1024 * 1024),
        **cost,
    )


def shape(*dims, dtype=f32):
    return jax.ShapeDtypeStruct(dims, dtype)


def iota(dims, axis):
    return lax.broadcasted_iota(jnp.int32, dims, axis)


def dot_nt(a, b):
    return lax.dot_general(a, b, (((1,), (1,)), ((), ())), preferred_element_type=f32)


def dot(a, b):
    return jnp.dot(a, b, preferred_element_type=f32)


def exchange(blocks, axes):
    return lax.all_to_all(blocks, axes, 0, 0)


def weight_kernel(core_ref, key_hbm, value_hbm, query_hbm, out_ref, key_ref, value_ref, query_ref, tile, sems):
    copies = [
        pltpu.make_async_copy(source, target, sems.at[index])
        for index, (source, target) in enumerate(
            ((query_hbm, query_ref), (key_hbm, key_ref), (value_hbm, value_ref))
        )
    ]
    for copy in copies:
        copy.start()
    members = jnp.where(iota((HEADS, D), 1) // HEAD_DIM == iota((HEADS, D), 0), 1.0, 0.0).astype(bf16)
    tile[...] = jnp.zeros_like(tile)
    for copy in copies:
        copy.wait()
    keys = key_ref[...].astype(f32)
    values = value_ref[...].astype(f32)
    query = query_ref[...].astype(f32)
    query = jnp.concatenate([query[row : row + 1] for row in range(TILES)], axis=1)
    products = keys * query
    high = products.astype(bf16)
    low = (products - high.astype(f32)).astype(bf16)
    folded = (dot_nt(high, members) + dot_nt(low, members)) * (1.0 / math.sqrt(HEAD_DIM))
    mine = core_ref[0] == 0
    half = HEADS // 2 * HEAD_DIM
    keys = jnp.where(mine, keys[:, :half], keys[:, half:])
    values = jnp.where(mine, values[:, :half], values[:, half:])
    for head in range(HEADS // 2):
        at = head * HEAD_DIM
        tile[:W_ROWS, :HEAD_DIM] = values[:, at : at + HEAD_DIM]
        tile[:W_ROWS, AT_FOLDED:AT_KEY] = folded
        tile[:W_ROWS, AT_KEY:] = keys[:, at : at + KEY_FIRST]
        for part in range(3):
            tile[W_ROWS:, part * KEY_REST : (part + 1) * KEY_REST] = keys[
                part * 6 : part * 6 + 6, at + KEY_FIRST : at + HEAD_DIM
            ]
        out_ref[head * 8 : head * 8 + 8] = jnp.broadcast_to(tile[...].astype(bf16)[None], (8, 24, 128))


def three_parts(value):
    first = value.astype(bf16).astype(f32)
    rest = value - first
    second = rest.astype(bf16).astype(f32)
    return first, second, rest - second


def context_kernel(
    weights_ref, patches_hbm, segments_hbm, tail_ref, out_ref, patches_ref, segments_ref, main, sums, sems
):
    step = ROWS // CHUNKS
    spans = [pl.ds(chunk * step, step) for chunk in range(CHUNKS)]
    copies = [
        pltpu.make_async_copy(patches_hbm.at[span], patches_ref.at[span], sems.at[chunk])
        for chunk, span in enumerate(spans)
    ]
    copies.append(pltpu.make_async_copy(segments_hbm, segments_ref, sems.at[CHUNKS]))
    for copy in copies:
        copy.start()
    for source in range(N_GRP):
        at = source * W_ROWS
        main[at : at + W_ROWS, :] = weights_ref[source].astype(f32)[:W_ROWS]
    folded = main[...].astype(bf16)
    scores = []
    for copy, span in zip(copies, spans):
        copy.wait()
        scores.append(dot(patches_ref[span, :], folded).T[AT_FOLDED:AT_KEY])
    scores = jnp.concatenate(scores, axis=1)
    copies[CHUNKS].wait()

    segments = segments_ref[...]
    masked = jnp.concatenate([jnp.where(segments == slot, scores, LOW) for slot in range(IMG_DEV)], axis=0)
    place = iota((IMG_DEV * HEADS, ROWS), 1)
    peak = jnp.max(masked, axis=1, keepdims=True)
    powers = jnp.where(masked > 0.5 * LOW, jnp.exp(masked - peak), 0.0)
    total = jnp.sum(powers, axis=1, keepdims=True)
    best = peak
    picks, values = [], []
    for top in range(TOPS):
        if top > 0:
            best = jnp.max(masked, axis=1, keepdims=True)
        there = best > 0.5 * LOW
        first = jnp.min(jnp.where(masked == best, place, ROWS), axis=1, keepdims=True)
        hit = (place == first) & there
        picks.append(jnp.where(hit, 1.0, 0.0).astype(bf16))
        masked = jnp.where(hit, LOW, masked)
        powers = jnp.where(hit, 0.0, powers)
        values.append(jnp.where(there, 1.0, 0.0))
    others = powers / total
    context = dot(jnp.concatenate([others.astype(bf16), *picks], axis=0), patches_ref[...])
    values = [
        *three_parts(peak + jnp.log(total)),
        *three_parts(jnp.sum(others, axis=1, keepdims=True)),
        *values,
    ]
    lanes = iota((IMG_DEV * HEADS, 128), 1) - iota((IMG_DEV * HEADS, 128), 0) // HEADS * N_LANES
    scalars = jnp.zeros((IMG_DEV * HEADS, 128), f32)
    for index, value in enumerate(values):
        scalars = jnp.where(lanes == index, value, scalars)
    scalars = scalars[:HEADS] + scalars[HEADS : 2 * HEADS] + scalars[2 * HEADS :]

    def put(row, value):
        sums[pl.ds(row, HEADS, stride=NEAR_ROWS), :] = value

    blank = jnp.zeros((HEADS, 128), f32)
    for tile in range(TILES):
        for row in range(AT_TEXT):
            put(tile * NEAR_LIST + row, context[row * HEADS : (row + 1) * HEADS, tile * 128 : (tile + 1) * 128])
        for row in range(AT_TEXT, NEAR_LIST):
            at = tile * NEAR_LIST + row
            put(at, scalars if at == AT_SCALAR else jnp.broadcast_to(tail_ref[at : at + 1, :], (HEADS, 128)))
    for row in range(TILES * NEAR_LIST, NEAR_ROWS):
        put(row, blank)
    out_ref[...] = sums[...].reshape(HEADS, NEAR_ROWS, 128).astype(bf16)


def project_kernel(place_ref, near_ref, weights_ref, query_ref, out_ref, text_ref, index_ref, rows, main, extra):
    for source in range(N_SIDE):
        rows[source * NEAR_ROWS : (source + 1) * NEAR_ROWS, :] = near_ref[source].astype(f32)
    for source in range(N_GRP):
        block = weights_ref[source].astype(f32)
        at = source * W_ROWS
        main[at : at + W_ROWS, :] = block[:W_ROWS]
        for part in range(3):
            extra[at + part * 6 : at + part * 6 + 6, :] = block[
                W_ROWS:, part * KEY_REST : (part + 1) * KEY_REST
            ]

    def take(row):
        return rows[pl.ds(row, N_SIDE, stride=NEAR_ROWS), :]

    near = jnp.concatenate(
        [
            jnp.concatenate([take(tile * NEAR_LIST + row) for row in range(AT_ID)], axis=0).astype(bf16)
            for tile in range(TILES)
        ],
        axis=1,
    )
    text_ref[...] = near[AT_TEXT * N_SIDE :]
    pair = jnp.concatenate([main[...], main[:, AT_KEY:], extra[...]], axis=1).astype(bf16)
    both = dot(near[: AT_TEXT * N_SIDE], pair)
    count = IMG_DEV * N_SIDE
    scalars = take(AT_SCALAR)
    lanes = iota((N_SIDE, 128), 1)

    def scalar(index):
        return jnp.concatenate(
            [
                jnp.sum(jnp.where(lanes == slot * N_LANES + index, scalars, 0.0), axis=1, keepdims=True)
                for slot in range(IMG_DEV)
            ],
            axis=0,
        )

    level = scalar(0) + scalar(1) + scalar(2)
    others = scalar(3) + scalar(4) + scalar(5)
    some = others > 0.0
    peak = jnp.where(some, 0.0, LOW)
    powers = []
    for top in range(TOPS):
        keys = both[(top + 1) * count : (top + 2) * count, 128:].astype(bf16).astype(f32)
        score = jnp.sum(keys * query_ref[...], axis=1, keepdims=True) / math.sqrt(HEAD_DIM)
        there = scalar(6 + top) > 0.5
        score = jnp.where(there, score - level, LOW)
        peak = jnp.maximum(peak, score)
        powers.append((there, score))
    powers = [jnp.where(there, jnp.exp(score - peak), 0.0) for there, score in powers]
    shift = jnp.where(some, jnp.exp(jnp.where(some, -peak, 0.0)), 0.0)
    total = others * shift
    for power in powers:
        total = total + power
    pooled = both[:count, :HEAD_DIM] * (shift / total)
    for top, power in enumerate(powers):
        value = both[(top + 1) * count : (top + 2) * count, :HEAD_DIM].astype(bf16).astype(f32)
        pooled = pooled + (power / total).astype(bf16).astype(f32) * value
    pooled = jnp.concatenate([pooled[slot * N_SIDE : (slot + 1) * N_SIDE] for slot in range(IMG_DEV)], axis=1)
    out_ref[...] = jnp.broadcast_to(pooled[None], out_ref.shape)

    ids = take(AT_NEAR_ID)
    member = iota((N_SIDE, 1), 0)
    for slot in range(IMG_DEV):
        text = ((place_ref[0] * N_SIDE + member) * 8 + place_ref[1]) * IMG_DEV + slot
        code = jnp.where(lanes == slot, float(ID_BASE), 0.0) + jnp.where(lanes == slot + IMG_DEV, 1.0, 0.0)
        image = jnp.sum(ids * code, axis=1, keepdims=True).astype(jnp.int32)
        index_ref[slot * N_SIDE : (slot + 1) * N_SIDE, :] = text
        index_ref[count + slot * N_SIDE : count + (slot + 1) * N_SIDE, :] = image


def unit_kernel(place_ref, pooled_ref, tail_ref, out_ref, low_ref, unit_ref, norm_ref, units, norms, block):
    side = place_ref[2]
    for slot in range(IMG_DEV):
        for head in range(HEADS):
            units[slot, :, head * HEAD_DIM : (head + 1) * HEAD_DIM] = pooled_ref[
                head, :, slot * HEAD_DIM : (slot + 1) * HEAD_DIM
            ]
    block[...] = tail_ref[...]

    def put(row, value):
        for tile in range(TILES):
            block[tile * 6 + row : tile * 6 + row + 1, :] = value[:, tile * 128 : (tile + 1) * 128]

    for slot in range(IMG_DEV):
        pooled = units[slot]
        norm = jnp.sqrt(jnp.sum(pooled * pooled, axis=1, keepdims=True) + EPS)
        unit = pooled / norm
        units[slot] = unit
        norms[slot] = jnp.broadcast_to(norm, (N_SIDE, 128))
        low_ref[slot * N_SIDE : (slot + 1) * N_SIDE, :] = unit.astype(bf16)
        own = units[slot, pl.ds(side, 1), :]
        put(slot, own)
        unit_ref[slot : slot + 1, :] = own
        norm_ref[slot : slot + 1, :] = norms[slot, pl.ds(side, 1), :]
    out_ref[...] = jnp.broadcast_to(block[...].astype(bf16)[None], out_ref.shape)


def pair_kernel(params_ref, place_ref, far_ref, text_ref, low_ref, index_ref, out_ref, far_rows, sums):
    scale, offset = params_ref[0], params_ref[1]
    for source in range(N_FAR):
        far_rows[source * FAR_ROWS : (source + 1) * FAR_ROWS, :] = far_ref[source].astype(f32)

    def take(row):
        return far_rows[pl.ds(row, N_FAR, stride=FAR_ROWS), :].astype(bf16)

    digit = iota((8, 128), 1)
    slot = iota((8, 128), 0)
    code = jnp.where(digit == slot, float(ID_BASE), 0.0) + jnp.where(digit == slot + IMG_DEV, 1.0, 0.0)
    ids = dot_nt(jnp.where(slot < IMG_DEV, code, 0.0).astype(bf16), take(AT_FAR_ID))
    ids = jnp.concatenate([ids[row : row + 1] for row in range(IMG_DEV)], axis=1).astype(jnp.int32)
    columns = IMG_DEV * N_FAR
    column = iota((1, columns), 1)
    device = column % N_FAR
    device = ((device // 8) * N_SIDE + place_ref[2]) * 8 + device % 8
    text_index = device * IMG_DEV + column // N_FAR
    sums[...] = jnp.zeros_like(sums)
    for first, near, index, place in ((0, text_ref[...], ids, 0), (IMG_DEV, low_ref[...], text_index, 1)):
        far = jnp.concatenate(
            [
                jnp.concatenate([take(tile * 6 + first + row) for row in range(IMG_DEV)], axis=0)
                for tile in range(TILES)
            ],
            axis=1,
        )
        logits = scale * dot_nt(near, far) + offset
        own = index_ref[place * IMG_DEV * N_SIDE : (place + 1) * IMG_DEV * N_SIDE, :]
        pair_sign = jnp.where(own == index, 1.0, -1.0)
        scaled = scale * (-pair_sign * jax.nn.sigmoid(-pair_sign * logits) / PAIRS)
        parts = dot(scaled.astype(bf16), far)
        for tile in range(TILES):
            for row in range(IMG_DEV):
                sums[pl.ds(tile * 6 + first + row, N_SIDE, stride=FAR_ROWS), :] = parts[
                    row * N_SIDE : (row + 1) * N_SIDE, tile * 128 : (tile + 1) * 128
                ]
    out_ref[...] = sums[...].reshape(N_SIDE, FAR_ROWS, 128).astype(bf16)


def final_kernel(parts_ref, unit_text_ref, text_norm_ref, unit_image_ref, image_norm_ref, image_ref, text_ref, sums):
    total = parts_ref[0].astype(f32)
    for source in range(1, N_SIDE):
        total = total + parts_ref[source].astype(f32)
    sums[...] = total
    whole = jnp.concatenate([sums[tile * 6 : tile * 6 + 6, :] for tile in range(TILES)], axis=1)
    for first, unit_ref, norm, out_ref in (
        (0, unit_text_ref, text_norm_ref[:, :1], text_ref),
        (IMG_DEV, unit_image_ref, image_norm_ref[:, :1], image_ref),
    ):
        part = whole[first : first + IMG_DEV]
        unit = unit_ref[...]
        out_ref[...] = (part - unit * jnp.sum(unit * part, axis=1, keepdims=True)) / norm


def tiled_rows(array):
    rows = array.shape[0]
    return jnp.transpose(array.reshape(rows, TILES, 128), (1, 0, 2))


def code_ids(ids):
    row = jnp.concatenate([ids // ID_BASE, ids % ID_BASE]).astype(f32)
    return jnp.pad(row, (0, 128 - 2 * IMG_DEV))[None]


def weight_messages(core, key_weight, value_weight, pool_query):
    return call(
        weight_kernel,
        [shape(N_GRP, 24, 128, dtype=bf16)],
        [
            pltpu.VMEM((W_ROWS, D), bf16),
            pltpu.VMEM((W_ROWS, D), bf16),
            pltpu.VMEM((TILES, 128), bf16),
            pltpu.VMEM((24, 128), f32),
            pltpu.SemaphoreType.DMA((3,)),
        ],
        limit=62,
        in_specs=[SMEM, ANY, ANY, ANY],
    )(core, key_weight, value_weight, pool_query.reshape(TILES, 128))


def context_messages(weights, patches, segments, tail):
    return call(
        context_kernel,
        [shape(HEADS, NEAR_ROWS, 128, dtype=bf16)],
        [
            pltpu.VMEM((ROWS, D), bf16),
            pltpu.VMEM((1, ROWS), jnp.int32),
            pltpu.VMEM((D, 128), f32),
            pltpu.VMEM((HEADS * NEAR_ROWS, 128), f32),
            pltpu.SemaphoreType.DMA((CHUNKS + 1,)),
        ],
        limit=52,
        in_specs=[VMEM, ANY, ANY, VMEM],
    )(weights, patches, segments, tail)


def pooled_messages(place, near, weights, query):
    return call(
        project_kernel,
        [
            shape(N_SIDE, N_SIDE, IMG_DEV * HEAD_DIM),
            shape(IMG_DEV * N_SIDE, D, dtype=bf16),
            shape(2 * IMG_DEV * N_SIDE, 1, dtype=jnp.int32),
        ],
        [
            pltpu.VMEM((N_SIDE * NEAR_ROWS, 128), f32),
            pltpu.VMEM((D, 128), f32),
            pltpu.VMEM((D, KEY_REST), f32),
        ],
        in_specs=[SMEM] + [VMEM] * 3,
    )(place, near, weights, query)


def unit_messages(place, pooled, tail):
    return call(
        unit_kernel,
        [
            shape(N_FAR, FAR_ROWS, 128, dtype=bf16),
            shape(IMG_DEV * N_SIDE, D, dtype=bf16),
            shape(IMG_DEV, D),
            shape(IMG_DEV, 128),
        ],
        [pltpu.VMEM((IMG_DEV, N_SIDE, D), f32), pltpu.VMEM((IMG_DEV, N_SIDE, 128), f32), pltpu.VMEM((FAR_ROWS, 128), f32)],
        in_specs=[SMEM, VMEM, VMEM],
    )(place, pooled, tail)


def pair_messages(params, place, far, texts, lows, index):
    return call(
        pair_kernel,
        [shape(N_SIDE, FAR_ROWS, 128, dtype=bf16)],
        [pltpu.VMEM((N_FAR * FAR_ROWS, 128), f32), pltpu.VMEM((N_SIDE * FAR_ROWS, 128), f32)],
        in_specs=[SMEM, SMEM, VMEM, VMEM, VMEM, VMEM],
    )(params, place, far, texts, lows, index)


def gradients(parts, unit_text, text_norm, unit_image, image_norm):
    return call(
        final_kernel,
        [shape(IMG_DEV, D), shape(IMG_DEV, D)],
        [pltpu.VMEM((FAR_ROWS, 128), f32)],
        in_specs=[VMEM] * 5,
    )(parts, unit_text, text_norm, unit_image, image_norm)


def body(
    patches,
    segment_ids,
    image_ids,
    text_embeds,
    key_weight,
    value_weight,
    pool_query,
    logit_scale,
    logit_bias,
):
    yh, core, yl, x, z = (lax.axis_index(name) for name in FINE)
    side = (core * 2 + yl) * 4 + x
    weights = exchange(weight_messages(core[None], key_weight, value_weight, pool_query), GRP)

    text_full = text_embeds.astype(f32)
    text_norm = jnp.sqrt(jnp.sum(text_full * text_full, axis=1, keepdims=True) + EPS)
    unit_text = text_full / text_norm
    text_norm = jnp.broadcast_to(text_norm, (IMG_DEV, 128))
    text_low = tiled_rows(lax.reduce_precision(unit_text, 8, 7))
    ids = code_ids(image_ids)
    near_tail = jnp.pad(text_low, ((0, 0), (AT_TEXT, 1), (0, 0))).reshape(TILES * NEAR_LIST, 128)
    near_tail = jnp.where(jnp.arange(TILES * NEAR_LIST)[:, None] == AT_NEAR_ID, ids, near_tail)
    far_tail = jnp.pad(text_low, ((0, 0), (IMG_DEV, 0), (0, 0))).reshape(6 * TILES, 128)
    far_tail = jnp.concatenate([far_tail, ids, jnp.zeros((1, 128), f32)], axis=0)
    query = lax.dynamic_slice_in_dim(pool_query, side * HEAD_DIM, HEAD_DIM)[None].astype(f32)
    params = jnp.concatenate([logit_scale, logit_bias])
    place = jnp.stack([yh, z, side])
    weights, near_tail, far_tail, query, params, place, unit_text, text_norm = lax.optimization_barrier(
        (weights, near_tail, far_tail, query, params, place, unit_text, text_norm)
    )

    near = exchange(context_messages(weights, patches, segment_ids, near_tail), SIDE)
    pooled, texts, index = pooled_messages(place, near, weights, query)
    pooled = exchange(pooled, SIDE)
    far, lows, unit_image, image_norm = unit_messages(place, pooled, far_tail)
    far = exchange(far, FAR)
    parts = exchange(pair_messages(params, place, far, texts, lows, index), SIDE)
    return gradients(parts, unit_text, text_norm, unit_image, image_norm)


def solution(mesh):
    fine = Mesh(mesh.devices.reshape(FINE_SHAPE), FINE)
    rows = P(FINE, None)
    in_specs = (rows, rows, P(FINE), rows, P(GRP, None), P(GRP, None), P(), P(), P())
    return jax.shard_map(
        body, mesh=fine, in_specs=in_specs, out_specs=(rows, rows), check_vma=False
    )
```

```python
import math

import jax
import jax.numpy as jnp
from jax import lax
from jax.experimental import pallas as pl
from jax.experimental.pallas import tpu as pltpu
from jax.sharding import Mesh
from jax.sharding import PartitionSpec as P

D = 1152
TILES = D // 128
HEADS = 16
HEAD_DIM = 72
IMG_DEV = 3
PAIRS = 1536
EPS = 1e-06
ID_BASE = 64
ROWS = 768
LOW = -1e30

FINE = ("yh", "core", "yl", "x", "z")
FINE_SHAPE = (4, 2, 2, 4, 8)
SIDE = ("core", "yl", "x")
FAR = ("yh", "z")
GRP = ("yl", "x", "z")
N_SIDE = 16
N_FAR = 32
N_GRP = 64
W_ROWS = 18

AT_FOLDED = HEAD_DIM
AT_KEY = AT_FOLDED + HEADS
KEY_FIRST = 128 - AT_KEY
KEY_REST = HEAD_DIM - KEY_FIRST

TOPS = 2
AT_TOP = IMG_DEV
AT_TEXT = AT_TOP + TOPS * IMG_DEV
AT_ID = AT_TEXT + IMG_DEV
NEAR_LIST = AT_ID + 1
NEAR_ROWS = 120
AT_NEAR_ID = AT_ID
AT_SCALAR = NEAR_LIST + AT_ID
N_LANES = 8

AT_FAR_ID = 6 * TILES
FAR_ROWS = 56

f32 = jnp.float32
bf16 = jnp.bfloat16
VMEM = pl.BlockSpec(memory_space=pltpu.VMEM)
ANY = pl.BlockSpec(memory_space=pltpu.HBM)
SMEM = pl.BlockSpec(memory_space=pltpu.SMEM)


def call(kernel, outs, scratch=(), limit=40, **cost):
    many = len(outs) > 1
    return pl.pallas_call(
        kernel,
        out_shape=tuple(outs) if many else outs[0],
        out_specs=(VMEM,) * len(outs) if many else VMEM,
        scratch_shapes=list(scratch),
        compiler_params=pltpu.CompilerParams(vmem_limit_bytes=limit * 1024 * 1024),
        **cost,
    )


def shape(*dims, dtype=f32):
    return jax.ShapeDtypeStruct(dims, dtype)


def iota(dims, axis):
    return lax.broadcasted_iota(jnp.int32, dims, axis)


def dot_nt(a, b):
    return lax.dot_general(a, b, (((1,), (1,)), ((), ())), preferred_element_type=f32)


def dot(a, b):
    return jnp.dot(a, b, preferred_element_type=f32)


def exchange(blocks, axes):
    return lax.all_to_all(blocks, axes, 0, 0)


def weight_kernel(core_ref, key_hbm, value_hbm, query_hbm, out_ref, key_ref, value_ref, query_ref, tile, sems):
    copies = [
        pltpu.make_async_copy(source, target, sems.at[index])
        for index, (source, target) in enumerate(
            ((query_hbm, query_ref), (key_hbm, key_ref), (value_hbm, value_ref))
        )
    ]
    for copy in copies:
        copy.start()
    members = jnp.where(iota((HEADS, D), 1) // HEAD_DIM == iota((HEADS, D), 0), 1.0, 0.0).astype(bf16)
    tile[...] = jnp.zeros_like(tile)
    for copy in copies:
        copy.wait()
    keys = key_ref[...].astype(f32)
    values = value_ref[...].astype(f32)
    query = query_ref[...].astype(f32)
    query = jnp.concatenate([query[row : row + 1] for row in range(TILES)], axis=1)
    products = keys * query
    high = products.astype(bf16)
    low = (products - high.astype(f32)).astype(bf16)
    folded = (dot_nt(high, members) + dot_nt(low, members)) * (1.0 / math.sqrt(HEAD_DIM))
    mine = core_ref[0] == 0
    half = HEADS // 2 * HEAD_DIM
    keys = jnp.where(mine, keys[:, :half], keys[:, half:])
    values = jnp.where(mine, values[:, :half], values[:, half:])
    for head in range(HEADS // 2):
        at = head * HEAD_DIM
        tile[:W_ROWS, :HEAD_DIM] = values[:, at : at + HEAD_DIM]
        tile[:W_ROWS, AT_FOLDED:AT_KEY] = folded
        tile[:W_ROWS, AT_KEY:] = keys[:, at : at + KEY_FIRST]
        for part in range(3):
            tile[W_ROWS:, part * KEY_REST : (part + 1) * KEY_REST] = keys[
                part * 6 : part * 6 + 6, at + KEY_FIRST : at + HEAD_DIM
            ]
        out_ref[head * 8 : head * 8 + 8] = jnp.broadcast_to(tile[...].astype(bf16)[None], (8, 24, 128))


def three_parts(value):
    first = value.astype(bf16).astype(f32)
    rest = value - first
    second = rest.astype(bf16).astype(f32)
    return first, second, rest - second


def context_kernel(weights_ref, patches_ref, segments_ref, tail_ref, out_ref, main, sums):
    for source in range(N_GRP):
        at = source * W_ROWS
        main[at : at + W_ROWS, :] = weights_ref[source].astype(f32)[:W_ROWS]
    scores = dot(patches_ref[...], main[...].astype(bf16)).T[AT_FOLDED:AT_KEY]

    segments = segments_ref[...]
    masked = jnp.concatenate([jnp.where(segments == slot, scores, LOW) for slot in range(IMG_DEV)], axis=0)
    place = iota((IMG_DEV * HEADS, ROWS), 1)
    peak = jnp.max(masked, axis=1, keepdims=True)
    powers = jnp.where(masked > 0.5 * LOW, jnp.exp(masked - peak), 0.0)
    total = jnp.sum(powers, axis=1, keepdims=True)
    best = peak
    picks, values = [], []
    for top in range(TOPS):
        if top > 0:
            best = jnp.max(masked, axis=1, keepdims=True)
        there = best > 0.5 * LOW
        first = jnp.min(jnp.where(masked == best, place, ROWS), axis=1, keepdims=True)
        hit = (place == first) & there
        picks.append(jnp.where(hit, 1.0, 0.0).astype(bf16))
        masked = jnp.where(hit, LOW, masked)
        powers = jnp.where(hit, 0.0, powers)
        values.append(jnp.where(there, 1.0, 0.0))
    others = powers / total
    context = dot(jnp.concatenate([others.astype(bf16), *picks], axis=0), patches_ref[...])
    values = [
        *three_parts(peak + jnp.log(total)),
        *three_parts(jnp.sum(others, axis=1, keepdims=True)),
        *values,
    ]
    lanes = iota((IMG_DEV * HEADS, 128), 1) - iota((IMG_DEV * HEADS, 128), 0) // HEADS * N_LANES
    scalars = jnp.zeros((IMG_DEV * HEADS, 128), f32)
    for index, value in enumerate(values):
        scalars = jnp.where(lanes == index, value, scalars)
    scalars = scalars[:HEADS] + scalars[HEADS : 2 * HEADS] + scalars[2 * HEADS :]

    def put(row, value):
        sums[pl.ds(row, HEADS, stride=NEAR_ROWS), :] = value

    blank = jnp.zeros((HEADS, 128), f32)
    for tile in range(TILES):
        for row in range(AT_TEXT):
            put(tile * NEAR_LIST + row, context[row * HEADS : (row + 1) * HEADS, tile * 128 : (tile + 1) * 128])
        for row in range(AT_TEXT, NEAR_LIST):
            at = tile * NEAR_LIST + row
            put(at, scalars if at == AT_SCALAR else jnp.broadcast_to(tail_ref[at : at + 1, :], (HEADS, 128)))
    for row in range(TILES * NEAR_LIST, NEAR_ROWS):
        put(row, blank)
    out_ref[...] = sums[...].reshape(HEADS, NEAR_ROWS, 128).astype(bf16)


def project_kernel(place_ref, near_ref, weights_ref, query_ref, out_ref, text_ref, index_ref, rows, main, extra):
    for source in range(N_SIDE):
        rows[source * NEAR_ROWS : (source + 1) * NEAR_ROWS, :] = near_ref[source].astype(f32)
    for source in range(N_GRP):
        block = weights_ref[source].astype(f32)
        at = source * W_ROWS
        main[at : at + W_ROWS, :] = block[:W_ROWS]
        for part in range(3):
            extra[at + part * 6 : at + part * 6 + 6, :] = block[
                W_ROWS:, part * KEY_REST : (part + 1) * KEY_REST
            ]

    def take(row):
        return rows[pl.ds(row, N_SIDE, stride=NEAR_ROWS), :]

    near = jnp.concatenate(
        [
            jnp.concatenate([take(tile * NEAR_LIST + row) for row in range(AT_ID)], axis=0).astype(bf16)
            for tile in range(TILES)
        ],
        axis=1,
    )
    text_ref[...] = near[AT_TEXT * N_SIDE :]
    pair = jnp.concatenate([main[...], main[:, AT_KEY:], extra[...]], axis=1).astype(bf16)
    both = dot(near[: AT_TEXT * N_SIDE], pair)
    count = IMG_DEV * N_SIDE
    scalars = take(AT_SCALAR)
    lanes = iota((N_SIDE, 128), 1)

    def scalar(index):
        return jnp.concatenate(
            [
                jnp.sum(jnp.where(lanes == slot * N_LANES + index, scalars, 0.0), axis=1, keepdims=True)
                for slot in range(IMG_DEV)
            ],
            axis=0,
        )

    level = scalar(0) + scalar(1) + scalar(2)
    others = scalar(3) + scalar(4) + scalar(5)
    some = others > 0.0
    peak = jnp.where(some, 0.0, LOW)
    powers = []
    for top in range(TOPS):
        keys = both[(top + 1) * count : (top + 2) * count, 128:].astype(bf16).astype(f32)
        score = jnp.sum(keys * query_ref[...], axis=1, keepdims=True) / math.sqrt(HEAD_DIM)
        there = scalar(6 + top) > 0.5
        score = jnp.where(there, score - level, LOW)
        peak = jnp.maximum(peak, score)
        powers.append((there, score))
    powers = [jnp.where(there, jnp.exp(score - peak), 0.0) for there, score in powers]
    shift = jnp.where(some, jnp.exp(jnp.where(some, -peak, 0.0)), 0.0)
    total = others * shift
    for power in powers:
        total = total + power
    pooled = both[:count, :HEAD_DIM] * (shift / total)
    for top, power in enumerate(powers):
        value = both[(top + 1) * count : (top + 2) * count, :HEAD_DIM].astype(bf16).astype(f32)
        pooled = pooled + (power / total).astype(bf16).astype(f32) * value
    pooled = jnp.concatenate([pooled[slot * N_SIDE : (slot + 1) * N_SIDE] for slot in range(IMG_DEV)], axis=1)
    out_ref[...] = jnp.broadcast_to(pooled[None], out_ref.shape)

    ids = take(AT_NEAR_ID)
    member = iota((N_SIDE, 1), 0)
    for slot in range(IMG_DEV):
        text = ((place_ref[0] * N_SIDE + member) * 8 + place_ref[1]) * IMG_DEV + slot
        code = jnp.where(lanes == slot, float(ID_BASE), 0.0) + jnp.where(lanes == slot + IMG_DEV, 1.0, 0.0)
        image = jnp.sum(ids * code, axis=1, keepdims=True).astype(jnp.int32)
        index_ref[slot * N_SIDE : (slot + 1) * N_SIDE, :] = text
        index_ref[count + slot * N_SIDE : count + (slot + 1) * N_SIDE, :] = image


def unit_kernel(place_ref, pooled_ref, tail_ref, out_ref, low_ref, unit_ref, norm_ref, units, norms, block):
    side = place_ref[2]
    for slot in range(IMG_DEV):
        for head in range(HEADS):
            units[slot, :, head * HEAD_DIM : (head + 1) * HEAD_DIM] = pooled_ref[
                head, :, slot * HEAD_DIM : (slot + 1) * HEAD_DIM
            ]
    block[...] = tail_ref[...]

    def put(row, value):
        for tile in range(TILES):
            block[tile * 6 + row : tile * 6 + row + 1, :] = value[:, tile * 128 : (tile + 1) * 128]

    for slot in range(IMG_DEV):
        pooled = units[slot]
        norm = jnp.sqrt(jnp.sum(pooled * pooled, axis=1, keepdims=True) + EPS)
        unit = pooled / norm
        units[slot] = unit
        norms[slot] = jnp.broadcast_to(norm, (N_SIDE, 128))
        low_ref[slot * N_SIDE : (slot + 1) * N_SIDE, :] = unit.astype(bf16)
        own = units[slot, pl.ds(side, 1), :]
        put(slot, own)
        unit_ref[slot : slot + 1, :] = own
        norm_ref[slot : slot + 1, :] = norms[slot, pl.ds(side, 1), :]
    out_ref[...] = jnp.broadcast_to(block[...].astype(bf16)[None], out_ref.shape)


def pair_kernel(params_ref, place_ref, far_ref, text_ref, low_ref, index_ref, out_ref, far_rows, sums):
    scale, offset = params_ref[0], params_ref[1]
    for source in range(N_FAR):
        far_rows[source * FAR_ROWS : (source + 1) * FAR_ROWS, :] = far_ref[source].astype(f32)

    def take(row):
        return far_rows[pl.ds(row, N_FAR, stride=FAR_ROWS), :].astype(bf16)

    digit = iota((8, 128), 1)
    slot = iota((8, 128), 0)
    code = jnp.where(digit == slot, float(ID_BASE), 0.0) + jnp.where(digit == slot + IMG_DEV, 1.0, 0.0)
    ids = dot_nt(jnp.where(slot < IMG_DEV, code, 0.0).astype(bf16), take(AT_FAR_ID))
    ids = jnp.concatenate([ids[row : row + 1] for row in range(IMG_DEV)], axis=1).astype(jnp.int32)
    columns = IMG_DEV * N_FAR
    column = iota((1, columns), 1)
    device = column % N_FAR
    device = ((device // 8) * N_SIDE + place_ref[2]) * 8 + device % 8
    text_index = device * IMG_DEV + column // N_FAR
    sums[...] = jnp.zeros_like(sums)
    for first, near, index, place in ((0, text_ref[...], ids, 0), (IMG_DEV, low_ref[...], text_index, 1)):
        far = jnp.concatenate(
            [
                jnp.concatenate([take(tile * 6 + first + row) for row in range(IMG_DEV)], axis=0)
                for tile in range(TILES)
            ],
            axis=1,
        )
        logits = scale * dot_nt(near, far) + offset
        own = index_ref[place * IMG_DEV * N_SIDE : (place + 1) * IMG_DEV * N_SIDE, :]
        pair_sign = jnp.where(own == index, 1.0, -1.0)
        scaled = scale * (-pair_sign * jax.nn.sigmoid(-pair_sign * logits) / PAIRS)
        parts = dot(scaled.astype(bf16), far)
        for tile in range(TILES):
            for row in range(IMG_DEV):
                sums[pl.ds(tile * 6 + first + row, N_SIDE, stride=FAR_ROWS), :] = parts[
                    row * N_SIDE : (row + 1) * N_SIDE, tile * 128 : (tile + 1) * 128
                ]
    out_ref[...] = sums[...].reshape(N_SIDE, FAR_ROWS, 128).astype(bf16)


def final_kernel(parts_ref, unit_text_ref, text_norm_ref, unit_image_ref, image_norm_ref, image_ref, text_ref, sums):
    total = parts_ref[0].astype(f32)
    for source in range(1, N_SIDE):
        total = total + parts_ref[source].astype(f32)
    sums[...] = total
    whole = jnp.concatenate([sums[tile * 6 : tile * 6 + 6, :] for tile in range(TILES)], axis=1)
    for first, unit_ref, norm, out_ref in (
        (0, unit_text_ref, text_norm_ref[:, :1], text_ref),
        (IMG_DEV, unit_image_ref, image_norm_ref[:, :1], image_ref),
    ):
        part = whole[first : first + IMG_DEV]
        unit = unit_ref[...]
        out_ref[...] = (part - unit * jnp.sum(unit * part, axis=1, keepdims=True)) / norm


def tiled_rows(array):
    rows = array.shape[0]
    return jnp.transpose(array.reshape(rows, TILES, 128), (1, 0, 2))


def code_ids(ids):
    row = jnp.concatenate([ids // ID_BASE, ids % ID_BASE]).astype(f32)
    return jnp.pad(row, (0, 128 - 2 * IMG_DEV))[None]


def weight_messages(core, key_weight, value_weight, pool_query):
    return call(
        weight_kernel,
        [shape(N_GRP, 24, 128, dtype=bf16)],
        [
            pltpu.VMEM((W_ROWS, D), bf16),
            pltpu.VMEM((W_ROWS, D), bf16),
            pltpu.VMEM((TILES, 128), bf16),
            pltpu.VMEM((24, 128), f32),
            pltpu.SemaphoreType.DMA((3,)),
        ],
        limit=62,
        in_specs=[SMEM, ANY, ANY, ANY],
    )(core, key_weight, value_weight, pool_query.reshape(TILES, 128))


def fetch_kernel(patches_hbm, segments_hbm, patches_ref, segments_ref, sems):
    copies = [
        pltpu.make_async_copy(patches_hbm, patches_ref, sems.at[0]),
        pltpu.make_async_copy(segments_hbm, segments_ref, sems.at[1]),
    ]
    for copy in copies:
        copy.start()
    for copy in copies:
        copy.wait()


def fetch(patches, segments):
    return call(
        fetch_kernel,
        [shape(ROWS, D, dtype=bf16), shape(1, ROWS, dtype=jnp.int32)],
        [pltpu.SemaphoreType.DMA((2,))],
        limit=51,
        in_specs=[ANY, ANY],
    )(patches, segments)


def context_messages(weights, patches, segments, tail):
    return call(
        context_kernel,
        [shape(HEADS, NEAR_ROWS, 128, dtype=bf16)],
        [pltpu.VMEM((D, 128), f32), pltpu.VMEM((HEADS * NEAR_ROWS, 128), f32)],
        in_specs=[VMEM] * 4,
    )(weights, patches, segments, tail)


def pooled_messages(place, near, weights, query):
    return call(
        project_kernel,
        [
            shape(N_SIDE, N_SIDE, IMG_DEV * HEAD_DIM),
            shape(IMG_DEV * N_SIDE, D, dtype=bf16),
            shape(2 * IMG_DEV * N_SIDE, 1, dtype=jnp.int32),
        ],
        [
            pltpu.VMEM((N_SIDE * NEAR_ROWS, 128), f32),
            pltpu.VMEM((D, 128), f32),
            pltpu.VMEM((D, KEY_REST), f32),
        ],
        in_specs=[SMEM] + [VMEM] * 3,
    )(place, near, weights, query)


def unit_messages(place, pooled, tail):
    return call(
        unit_kernel,
        [
            shape(N_FAR, FAR_ROWS, 128, dtype=bf16),
            shape(IMG_DEV * N_SIDE, D, dtype=bf16),
            shape(IMG_DEV, D),
            shape(IMG_DEV, 128),
        ],
        [pltpu.VMEM((IMG_DEV, N_SIDE, D), f32), pltpu.VMEM((IMG_DEV, N_SIDE, 128), f32), pltpu.VMEM((FAR_ROWS, 128), f32)],
        in_specs=[SMEM, VMEM, VMEM],
    )(place, pooled, tail)


def pair_messages(params, place, far, texts, lows, index):
    return call(
        pair_kernel,
        [shape(N_SIDE, FAR_ROWS, 128, dtype=bf16)],
        [pltpu.VMEM((N_FAR * FAR_ROWS, 128), f32), pltpu.VMEM((N_SIDE * FAR_ROWS, 128), f32)],
        in_specs=[SMEM, SMEM, VMEM, VMEM, VMEM, VMEM],
    )(params, place, far, texts, lows, index)


def gradients(parts, unit_text, text_norm, unit_image, image_norm):
    return call(
        final_kernel,
        [shape(IMG_DEV, D), shape(IMG_DEV, D)],
        [pltpu.VMEM((FAR_ROWS, 128), f32)],
        in_specs=[VMEM] * 5,
    )(parts, unit_text, text_norm, unit_image, image_norm)


def body(
    patches,
    segment_ids,
    image_ids,
    text_embeds,
    key_weight,
    value_weight,
    pool_query,
    logit_scale,
    logit_bias,
):
    yh, core, yl, x, z = (lax.axis_index(name) for name in FINE)
    side = (core * 2 + yl) * 4 + x
    weights = exchange(weight_messages(core[None], key_weight, value_weight, pool_query), GRP)

    text_full = text_embeds.astype(f32)
    text_norm = jnp.sqrt(jnp.sum(text_full * text_full, axis=1, keepdims=True) + EPS)
    unit_text = text_full / text_norm
    text_norm = jnp.broadcast_to(text_norm, (IMG_DEV, 128))
    text_low = tiled_rows(lax.reduce_precision(unit_text, 8, 7))
    ids = code_ids(image_ids)
    near_tail = jnp.pad(text_low, ((0, 0), (AT_TEXT, 1), (0, 0))).reshape(TILES * NEAR_LIST, 128)
    near_tail = jnp.where(jnp.arange(TILES * NEAR_LIST)[:, None] == AT_NEAR_ID, ids, near_tail)
    far_tail = jnp.pad(text_low, ((0, 0), (IMG_DEV, 0), (0, 0))).reshape(6 * TILES, 128)
    far_tail = jnp.concatenate([far_tail, ids, jnp.zeros((1, 128), f32)], axis=0)
    query = lax.dynamic_slice_in_dim(pool_query, side * HEAD_DIM, HEAD_DIM)[None].astype(f32)
    patches, segments = fetch(patches, segment_ids)
    params = jnp.concatenate([logit_scale, logit_bias])
    place = jnp.stack([yh, z, side])
    weights, near_tail, far_tail, query, params, place, unit_text, text_norm = lax.optimization_barrier(
        (weights, near_tail, far_tail, query, params, place, unit_text, text_norm)
    )

    near = exchange(context_messages(weights, patches, segments, near_tail), SIDE)
    pooled, texts, index = pooled_messages(place, near, weights, query)
    pooled = exchange(pooled, SIDE)
    far, lows, unit_image, image_norm = unit_messages(place, pooled, far_tail)
    far = exchange(far, FAR)
    parts = exchange(pair_messages(params, place, far, texts, lows, index), SIDE)
    return gradients(parts, unit_text, text_norm, unit_image, image_norm)


def solution(mesh):
    fine = Mesh(mesh.devices.reshape(FINE_SHAPE), FINE)
    rows = P(FINE, None)
    in_specs = (rows, rows, P(FINE), rows, P(GRP, None), P(GRP, None), P(), P(), P())
    return jax.shard_map(
        body, mesh=fine, in_specs=in_specs, out_specs=(rows, rows), check_vma=False
    )
```

```python
import math

import jax
import jax.numpy as jnp
from jax import lax
from jax.experimental import pallas as pl
from jax.experimental.pallas import tpu as pltpu
from jax.sharding import Mesh
from jax.sharding import PartitionSpec as P

D = 1152
TILES = D // 128
HEADS = 16
HEAD_DIM = 72
IMG_DEV = 3
PAIRS = 1536
EPS = 1e-06
ID_BASE = 64
ROWS = 768
LOW = -1e30

FINE = ("yh", "core", "yl", "x", "z")
FINE_SHAPE = (4, 2, 2, 4, 8)
SIDE = ("core", "yl", "x")
FAR = ("yh", "z")
GRP = ("yl", "x", "z")
N_SIDE = 16
N_FAR = 32
N_GRP = 64
W_ROWS = 18

AT_FOLDED = HEAD_DIM
AT_KEY = AT_FOLDED + HEADS
KEY_FIRST = 128 - AT_KEY
KEY_REST = HEAD_DIM - KEY_FIRST

TOPS = 2
AT_TOP = IMG_DEV
AT_TEXT = AT_TOP + TOPS * IMG_DEV
AT_ID = AT_TEXT + IMG_DEV
NEAR_LIST = AT_ID + 1
NEAR_ROWS = 120
AT_NEAR_ID = AT_ID
AT_SCALAR = NEAR_LIST + AT_ID
N_LANES = 8

AT_FAR_ID = 6 * TILES
FAR_ROWS = 56

f32 = jnp.float32
bf16 = jnp.bfloat16
VMEM = pl.BlockSpec(memory_space=pltpu.VMEM)
ANY = pl.BlockSpec(memory_space=pltpu.HBM)
SMEM = pl.BlockSpec(memory_space=pltpu.SMEM)


def call(kernel, outs, scratch=(), limit=40, **cost):
    many = len(outs) > 1
    return pl.pallas_call(
        kernel,
        out_shape=tuple(outs) if many else outs[0],
        out_specs=(VMEM,) * len(outs) if many else VMEM,
        scratch_shapes=list(scratch),
        compiler_params=pltpu.CompilerParams(vmem_limit_bytes=limit * 1024 * 1024),
        **cost,
    )


def shape(*dims, dtype=f32):
    return jax.ShapeDtypeStruct(dims, dtype)


def iota(dims, axis):
    return lax.broadcasted_iota(jnp.int32, dims, axis)


def dot_nt(a, b):
    return lax.dot_general(a, b, (((1,), (1,)), ((), ())), preferred_element_type=f32)


def dot(a, b):
    return jnp.dot(a, b, preferred_element_type=f32)


def exchange(blocks, axes):
    return lax.all_to_all(blocks, axes, 0, 0)


def weight_kernel(core_ref, key_hbm, value_hbm, query_hbm, out_ref, key_ref, value_ref, query_ref, tile, sems):
    copies = [
        pltpu.make_async_copy(source, target, sems.at[index])
        for index, (source, target) in enumerate(
            ((query_hbm, query_ref), (key_hbm, key_ref), (value_hbm, value_ref))
        )
    ]
    for copy in copies:
        copy.start()
    members = jnp.where(iota((HEADS, D), 1) // HEAD_DIM == iota((HEADS, D), 0), 1.0, 0.0).astype(bf16)
    tile[...] = jnp.zeros_like(tile)
    for copy in copies:
        copy.wait()
    keys = key_ref[...].astype(f32)
    values = value_ref[...].astype(f32)
    query = query_ref[...].astype(f32)
    query = jnp.concatenate([query[row : row + 1] for row in range(TILES)], axis=1)
    products = keys * query
    high = products.astype(bf16)
    low = (products - high.astype(f32)).astype(bf16)
    folded = (dot_nt(high, members) + dot_nt(low, members)) * (1.0 / math.sqrt(HEAD_DIM))
    mine = core_ref[0] == 0
    half = HEADS // 2 * HEAD_DIM
    keys = jnp.where(mine, keys[:, :half], keys[:, half:])
    values = jnp.where(mine, values[:, :half], values[:, half:])
    for head in range(HEADS // 2):
        at = head * HEAD_DIM
        tile[:W_ROWS, :HEAD_DIM] = values[:, at : at + HEAD_DIM]
        tile[:W_ROWS, AT_FOLDED:AT_KEY] = folded
        tile[:W_ROWS, AT_KEY:] = keys[:, at : at + KEY_FIRST]
        for part in range(3):
            tile[W_ROWS:, part * KEY_REST : (part + 1) * KEY_REST] = keys[
                part * 6 : part * 6 + 6, at + KEY_FIRST : at + HEAD_DIM
            ]
        out_ref[head * 8 : head * 8 + 8] = jnp.broadcast_to(tile[...].astype(bf16)[None], (8, 24, 128))


def three_parts(value):
    first = value.astype(bf16).astype(f32)
    rest = value - first
    second = rest.astype(bf16).astype(f32)
    return first, second, rest - second


def context_kernel(weights_ref, patches_ref, segments_ref, tail_ref, out_ref, main, sums):
    for source in range(N_GRP):
        at = source * W_ROWS
        main[at : at + W_ROWS, :] = weights_ref[source].astype(f32)[:W_ROWS]
    scores = dot_nt(main[...].T[AT_FOLDED:AT_KEY].astype(bf16), patches_ref[...])

    segments = segments_ref[...]
    masked = jnp.concatenate([jnp.where(segments == slot, scores, LOW) for slot in range(IMG_DEV)], axis=0)
    place = iota((IMG_DEV * HEADS, ROWS), 1)
    peak = jnp.max(masked, axis=1, keepdims=True)
    powers = jnp.where(masked > 0.5 * LOW, jnp.exp(masked - peak), 0.0)
    total = jnp.sum(powers, axis=1, keepdims=True)
    best = peak
    picks, values = [], []
    for top in range(TOPS):
        if top > 0:
            best = jnp.max(masked, axis=1, keepdims=True)
        there = best > 0.5 * LOW
        first = jnp.min(jnp.where(masked == best, place, ROWS), axis=1, keepdims=True)
        hit = (place == first) & there
        picks.append(jnp.where(hit, 1.0, 0.0).astype(bf16))
        masked = jnp.where(hit, LOW, masked)
        powers = jnp.where(hit, 0.0, powers)
        values.append(jnp.where(there, 1.0, 0.0))
    others = powers / total
    context = dot(jnp.concatenate([others.astype(bf16), *picks], axis=0), patches_ref[...])
    values = [
        *three_parts(peak + jnp.log(total)),
        *three_parts(jnp.sum(others, axis=1, keepdims=True)),
        *values,
    ]
    lanes = iota((IMG_DEV * HEADS, 128), 1) - iota((IMG_DEV * HEADS, 128), 0) // HEADS * N_LANES
    scalars = jnp.zeros((IMG_DEV * HEADS, 128), f32)
    for index, value in enumerate(values):
        scalars = jnp.where(lanes == index, value, scalars)
    scalars = scalars[:HEADS] + scalars[HEADS : 2 * HEADS] + scalars[2 * HEADS :]

    def put(row, value):
        sums[pl.ds(row, HEADS, stride=NEAR_ROWS), :] = value

    blank = jnp.zeros((HEADS, 128), f32)
    for tile in range(TILES):
        for row in range(AT_TEXT):
            put(tile * NEAR_LIST + row, context[row * HEADS : (row + 1) * HEADS, tile * 128 : (tile + 1) * 128])
        for row in range(AT_TEXT, NEAR_LIST):
            at = tile * NEAR_LIST + row
            put(at, scalars if at == AT_SCALAR else jnp.broadcast_to(tail_ref[at : at + 1, :], (HEADS, 128)))
    for row in range(TILES * NEAR_LIST, NEAR_ROWS):
        put(row, blank)
    out_ref[...] = sums[...].reshape(HEADS, NEAR_ROWS, 128).astype(bf16)


def project_kernel(place_ref, near_ref, weights_ref, query_ref, out_ref, text_ref, index_ref, rows, main, extra):
    for source in range(N_SIDE):
        rows[source * NEAR_ROWS : (source + 1) * NEAR_ROWS, :] = near_ref[source].astype(f32)
    for source in range(N_GRP):
        block = weights_ref[source].astype(f32)
        at = source * W_ROWS
        main[at : at + W_ROWS, :] = block[:W_ROWS]
        for part in range(3):
            extra[at + part * 6 : at + part * 6 + 6, :] = block[
                W_ROWS:, part * KEY_REST : (part + 1) * KEY_REST
            ]

    def take(row):
        return rows[pl.ds(row, N_SIDE, stride=NEAR_ROWS), :]

    near = jnp.concatenate(
        [
            jnp.concatenate([take(tile * NEAR_LIST + row) for row in range(AT_ID)], axis=0).astype(bf16)
            for tile in range(TILES)
        ],
        axis=1,
    )
    text_ref[...] = near[AT_TEXT * N_SIDE :]
    pair = jnp.concatenate([main[...], main[:, AT_KEY:], extra[...]], axis=1).astype(bf16)
    both = dot(near[: AT_TEXT * N_SIDE], pair)
    count = IMG_DEV * N_SIDE
    scalars = take(AT_SCALAR)
    lanes = iota((N_SIDE, 128), 1)

    def scalar(index):
        return jnp.concatenate(
            [
                jnp.sum(jnp.where(lanes == slot * N_LANES + index, scalars, 0.0), axis=1, keepdims=True)
                for slot in range(IMG_DEV)
            ],
            axis=0,
        )

    level = scalar(0) + scalar(1) + scalar(2)
    others = scalar(3) + scalar(4) + scalar(5)
    some = others > 0.0
    peak = jnp.where(some, 0.0, LOW)
    powers = []
    for top in range(TOPS):
        keys = both[(top + 1) * count : (top + 2) * count, 128:].astype(bf16).astype(f32)
        score = jnp.sum(keys * query_ref[...], axis=1, keepdims=True) / math.sqrt(HEAD_DIM)
        there = scalar(6 + top) > 0.5
        score = jnp.where(there, score - level, LOW)
        peak = jnp.maximum(peak, score)
        powers.append((there, score))
    powers = [jnp.where(there, jnp.exp(score - peak), 0.0) for there, score in powers]
    shift = jnp.where(some, jnp.exp(jnp.where(some, -peak, 0.0)), 0.0)
    total = others * shift
    for power in powers:
        total = total + power
    pooled = both[:count, :HEAD_DIM] * (shift / total)
    for top, power in enumerate(powers):
        value = both[(top + 1) * count : (top + 2) * count, :HEAD_DIM].astype(bf16).astype(f32)
        pooled = pooled + (power / total).astype(bf16).astype(f32) * value
    pooled = jnp.concatenate([pooled[slot * N_SIDE : (slot + 1) * N_SIDE] for slot in range(IMG_DEV)], axis=1)
    out_ref[...] = jnp.broadcast_to(pooled.astype(bf16)[None], out_ref.shape)

    ids = take(AT_NEAR_ID)
    member = iota((N_SIDE, 1), 0)
    for slot in range(IMG_DEV):
        text = ((place_ref[0] * N_SIDE + member) * 8 + place_ref[1]) * IMG_DEV + slot
        code = jnp.where(lanes == slot, float(ID_BASE), 0.0) + jnp.where(lanes == slot + IMG_DEV, 1.0, 0.0)
        image = jnp.sum(ids * code, axis=1, keepdims=True).astype(jnp.int32)
        index_ref[slot * N_SIDE : (slot + 1) * N_SIDE, :] = text
        index_ref[count + slot * N_SIDE : count + (slot + 1) * N_SIDE, :] = image


def unit_kernel(place_ref, pooled_ref, tail_ref, out_ref, low_ref, unit_ref, norm_ref, units, norms, block):
    side = place_ref[2]
    for head in range(HEADS):
        pooled = pooled_ref[head].astype(f32)
        for slot in range(IMG_DEV):
            units[slot, :, head * HEAD_DIM : (head + 1) * HEAD_DIM] = pooled[
                :, slot * HEAD_DIM : (slot + 1) * HEAD_DIM
            ]
    block[...] = tail_ref[...]

    def put(row, value):
        for tile in range(TILES):
            block[tile * 6 + row : tile * 6 + row + 1, :] = value[:, tile * 128 : (tile + 1) * 128]

    for slot in range(IMG_DEV):
        pooled = units[slot]
        norm = jnp.sqrt(jnp.sum(pooled * pooled, axis=1, keepdims=True) + EPS)
        unit = pooled / norm
        units[slot] = unit
        norms[slot] = jnp.broadcast_to(norm, (N_SIDE, 128))
        low_ref[slot * N_SIDE : (slot + 1) * N_SIDE, :] = unit.astype(bf16)
        own = units[slot, pl.ds(side, 1), :]
        put(slot, own)
        unit_ref[slot : slot + 1, :] = own
        norm_ref[slot : slot + 1, :] = norms[slot, pl.ds(side, 1), :]
    out_ref[...] = jnp.broadcast_to(block[...].astype(bf16)[None], out_ref.shape)


def pair_kernel(params_ref, place_ref, far_ref, text_ref, low_ref, index_ref, out_ref, far_rows, sums):
    scale, offset = params_ref[0], params_ref[1]
    for source in range(N_FAR):
        far_rows[source * FAR_ROWS : (source + 1) * FAR_ROWS, :] = far_ref[source].astype(f32)

    def take(row):
        return far_rows[pl.ds(row, N_FAR, stride=FAR_ROWS), :].astype(bf16)

    digit = iota((8, 128), 1)
    slot = iota((8, 128), 0)
    code = jnp.where(digit == slot, float(ID_BASE), 0.0) + jnp.where(digit == slot + IMG_DEV, 1.0, 0.0)
    ids = dot_nt(jnp.where(slot < IMG_DEV, code, 0.0).astype(bf16), take(AT_FAR_ID))
    ids = jnp.concatenate([ids[row : row + 1] for row in range(IMG_DEV)], axis=1).astype(jnp.int32)
    columns = IMG_DEV * N_FAR
    column = iota((1, columns), 1)
    device = column % N_FAR
    device = ((device // 8) * N_SIDE + place_ref[2]) * 8 + device % 8
    text_index = device * IMG_DEV + column // N_FAR
    sums[...] = jnp.zeros_like(sums)
    for first, near, index, place in ((0, text_ref[...], ids, 0), (IMG_DEV, low_ref[...], text_index, 1)):
        far = jnp.concatenate(
            [
                jnp.concatenate([take(tile * 6 + first + row) for row in range(IMG_DEV)], axis=0)
                for tile in range(TILES)
            ],
            axis=1,
        )
        logits = scale * dot_nt(near, far) + offset
        own = index_ref[place * IMG_DEV * N_SIDE : (place + 1) * IMG_DEV * N_SIDE, :]
        pair_sign = jnp.where(own == index, 1.0, -1.0)
        scaled = scale * (-pair_sign * jax.nn.sigmoid(-pair_sign * logits) / PAIRS)
        parts = dot(scaled.astype(bf16), far)
        for tile in range(TILES):
            for row in range(IMG_DEV):
                sums[pl.ds(tile * 6 + first + row, N_SIDE, stride=FAR_ROWS), :] = parts[
                    row * N_SIDE : (row + 1) * N_SIDE, tile * 128 : (tile + 1) * 128
                ]
    out_ref[...] = sums[...].reshape(N_SIDE, FAR_ROWS, 128).astype(bf16)


def final_kernel(parts_ref, unit_text_ref, text_norm_ref, unit_image_ref, image_norm_ref, image_ref, text_ref, sums):
    total = parts_ref[0].astype(f32)
    for source in range(1, N_SIDE):
        total = total + parts_ref[source].astype(f32)
    sums[...] = total
    whole = jnp.concatenate([sums[tile * 6 : tile * 6 + 6, :] for tile in range(TILES)], axis=1)
    for first, unit_ref, norm, out_ref in (
        (0, unit_text_ref, text_norm_ref[:, :1], text_ref),
        (IMG_DEV, unit_image_ref, image_norm_ref[:, :1], image_ref),
    ):
        part = whole[first : first + IMG_DEV]
        unit = unit_ref[...]
        out_ref[...] = (part - unit * jnp.sum(unit * part, axis=1, keepdims=True)) / norm


def tiled_rows(array):
    rows = array.shape[0]
    return jnp.transpose(array.reshape(rows, TILES, 128), (1, 0, 2))


def code_ids(ids):
    row = jnp.concatenate([ids // ID_BASE, ids % ID_BASE]).astype(f32)
    return jnp.pad(row, (0, 128 - 2 * IMG_DEV))[None]


def weight_messages(core, key_weight, value_weight, pool_query):
    return call(
        weight_kernel,
        [shape(N_GRP, 24, 128, dtype=bf16)],
        [
            pltpu.VMEM((W_ROWS, D), bf16),
            pltpu.VMEM((W_ROWS, D), bf16),
            pltpu.VMEM((TILES, 128), bf16),
            pltpu.VMEM((24, 128), f32),
            pltpu.SemaphoreType.DMA((3,)),
        ],
        limit=62,
        in_specs=[SMEM, ANY, ANY, ANY],
    )(core, key_weight, value_weight, pool_query.reshape(TILES, 128))


def fetch_kernel(patches_hbm, segments_hbm, patches_ref, segments_ref, sems):
    copies = [
        pltpu.make_async_copy(patches_hbm, patches_ref, sems.at[0]),
        pltpu.make_async_copy(segments_hbm, segments_ref, sems.at[1]),
    ]
    for copy in copies:
        copy.start()
    for copy in copies:
        copy.wait()


def fetch(patches, segments):
    return call(
        fetch_kernel,
        [shape(ROWS, D, dtype=bf16), shape(1, ROWS, dtype=jnp.int32)],
        [pltpu.SemaphoreType.DMA((2,))],
        limit=51,
        in_specs=[ANY, ANY],
    )(patches, segments)


def context_messages(weights, patches, segments, tail):
    return call(
        context_kernel,
        [shape(HEADS, NEAR_ROWS, 128, dtype=bf16)],
        [pltpu.VMEM((D, 128), f32), pltpu.VMEM((HEADS * NEAR_ROWS, 128), f32)],
        in_specs=[VMEM] * 4,
    )(weights, patches, segments, tail)


def pooled_messages(place, near, weights, query):
    return call(
        project_kernel,
        [
            shape(N_SIDE, N_SIDE, IMG_DEV * HEAD_DIM, dtype=bf16),
            shape(IMG_DEV * N_SIDE, D, dtype=bf16),
            shape(2 * IMG_DEV * N_SIDE, 1, dtype=jnp.int32),
        ],
        [
            pltpu.VMEM((N_SIDE * NEAR_ROWS, 128), f32),
            pltpu.VMEM((D, 128), f32),
            pltpu.VMEM((D, KEY_REST), f32),
        ],
        in_specs=[SMEM] + [VMEM] * 3,
    )(place, near, weights, query)


def unit_messages(place, pooled, tail):
    return call(
        unit_kernel,
        [
            shape(N_FAR, FAR_ROWS, 128, dtype=bf16),
            shape(IMG_DEV * N_SIDE, D, dtype=bf16),
            shape(IMG_DEV, D),
            shape(IMG_DEV, 128),
        ],
        [pltpu.VMEM((IMG_DEV, N_SIDE, D), f32), pltpu.VMEM((IMG_DEV, N_SIDE, 128), f32), pltpu.VMEM((FAR_ROWS, 128), f32)],
        in_specs=[SMEM, VMEM, VMEM],
    )(place, pooled, tail)


def pair_messages(params, place, far, texts, lows, index):
    return call(
        pair_kernel,
        [shape(N_SIDE, FAR_ROWS, 128, dtype=bf16)],
        [pltpu.VMEM((N_FAR * FAR_ROWS, 128), f32), pltpu.VMEM((N_SIDE * FAR_ROWS, 128), f32)],
        in_specs=[SMEM, SMEM, VMEM, VMEM, VMEM, VMEM],
    )(params, place, far, texts, lows, index)


def gradients(parts, unit_text, text_norm, unit_image, image_norm):
    return call(
        final_kernel,
        [shape(IMG_DEV, D), shape(IMG_DEV, D)],
        [pltpu.VMEM((FAR_ROWS, 128), f32)],
        in_specs=[VMEM] * 5,
    )(parts, unit_text, text_norm, unit_image, image_norm)


def body(
    patches,
    segment_ids,
    image_ids,
    text_embeds,
    key_weight,
    value_weight,
    pool_query,
    logit_scale,
    logit_bias,
):
    yh, core, yl, x, z = (lax.axis_index(name) for name in FINE)
    side = (core * 2 + yl) * 4 + x
    weights = exchange(weight_messages(core[None], key_weight, value_weight, pool_query), GRP)

    text_full = text_embeds.astype(f32)
    text_norm = jnp.sqrt(jnp.sum(text_full * text_full, axis=1, keepdims=True) + EPS)
    unit_text = text_full / text_norm
    text_norm = jnp.broadcast_to(text_norm, (IMG_DEV, 128))
    text_low = tiled_rows(lax.reduce_precision(unit_text, 8, 7))
    ids = code_ids(image_ids)
    near_tail = jnp.pad(text_low, ((0, 0), (AT_TEXT, 1), (0, 0))).reshape(TILES * NEAR_LIST, 128)
    near_tail = jnp.where(jnp.arange(TILES * NEAR_LIST)[:, None] == AT_NEAR_ID, ids, near_tail)
    far_tail = jnp.pad(text_low, ((0, 0), (IMG_DEV, 0), (0, 0))).reshape(6 * TILES, 128)
    far_tail = jnp.concatenate([far_tail, ids, jnp.zeros((1, 128), f32)], axis=0)
    query = lax.dynamic_slice_in_dim(pool_query, side * HEAD_DIM, HEAD_DIM)[None].astype(f32)
    patches, segments = fetch(patches, segment_ids)
    params = jnp.concatenate([logit_scale, logit_bias])
    place = jnp.stack([yh, z, side])
    weights, near_tail, far_tail, query, params, place, unit_text, text_norm = lax.optimization_barrier(
        (weights, near_tail, far_tail, query, params, place, unit_text, text_norm)
    )

    near = exchange(context_messages(weights, patches, segments, near_tail), SIDE)
    pooled, texts, index = pooled_messages(place, near, weights, query)
    pooled = exchange(pooled, SIDE)
    far, lows, unit_image, image_norm = unit_messages(place, pooled, far_tail)
    far = exchange(far, FAR)
    parts = exchange(pair_messages(params, place, far, texts, lows, index), SIDE)
    return gradients(parts, unit_text, text_norm, unit_image, image_norm)


def solution(mesh):
    fine = Mesh(mesh.devices.reshape(FINE_SHAPE), FINE)
    rows = P(FINE, None)
    in_specs = (rows, rows, P(FINE), rows, P(GRP, None), P(GRP, None), P(), P(), P())
    return jax.shard_map(
        body, mesh=fine, in_specs=in_specs, out_specs=(rows, rows), check_vma=False
    )
```

```python
import math

import jax
import jax.numpy as jnp
from jax import lax
from jax.experimental import pallas as pl
from jax.experimental.pallas import tpu as pltpu
from jax.sharding import Mesh
from jax.sharding import PartitionSpec as P

D = 1152
TILES = D // 128
HEADS = 16
HEAD_DIM = 72
IMG_DEV = 3
PAIRS = 1536
EPS = 1e-06
ID_BASE = 64
ROWS = 768
LOW = -1e30

FINE = ("yh", "core", "yl", "x", "z")
FINE_SHAPE = (4, 2, 2, 4, 8)
SIDE = ("core", "yl", "x")
GRP = ("yl", "x", "z")
N_SIDE = 16
N_FAR = 32
N_GRP = 64
W_ROWS = 18

AT_FOLDED = HEAD_DIM
AT_KEY = AT_FOLDED + HEADS
KEY_FIRST = 128 - AT_KEY
KEY_REST = HEAD_DIM - KEY_FIRST

TOPS = 2
AT_TOP = IMG_DEV
AT_TEXT = AT_TOP + TOPS * IMG_DEV
AT_ID = AT_TEXT + IMG_DEV
NEAR_LIST = AT_ID + 1
NEAR_ROWS = 120
AT_NEAR_ID = AT_ID
AT_SCALAR = NEAR_LIST + AT_ID
N_LANES = 8

AT_FAR_ID = 6 * TILES
FAR_ROWS = 56

f32 = jnp.float32
bf16 = jnp.bfloat16
VMEM = pl.BlockSpec(memory_space=pltpu.VMEM)
ANY = pl.BlockSpec(memory_space=pltpu.HBM)
SMEM = pl.BlockSpec(memory_space=pltpu.SMEM)


def call(kernel, outs, scratch=(), limit=40, **cost):
    many = len(outs) > 1
    return pl.pallas_call(
        kernel,
        out_shape=tuple(outs) if many else outs[0],
        out_specs=(VMEM,) * len(outs) if many else VMEM,
        scratch_shapes=list(scratch),
        compiler_params=pltpu.CompilerParams(vmem_limit_bytes=limit * 1024 * 1024),
        **cost,
    )


def shape(*dims, dtype=f32):
    return jax.ShapeDtypeStruct(dims, dtype)


def iota(dims, axis):
    return lax.broadcasted_iota(jnp.int32, dims, axis)


def dot_nt(a, b):
    return lax.dot_general(a, b, (((1,), (1,)), ((), ())), preferred_element_type=f32)


def dot(a, b):
    return jnp.dot(a, b, preferred_element_type=f32)


def exchange(blocks, axes):
    return lax.all_to_all(blocks, axes, 0, 0)


def far_exchange(blocks):
    snake = [yh * 128 + (z if yh % 2 == 0 else 7 - z) for yh in range(4) for z in range(8)]
    groups = [[far + side * 8 for far in snake] for side in range(N_SIDE)]
    return lax.all_to_all(blocks, FINE, 0, 0, axis_index_groups=groups)


def weight_kernel(core_ref, key_hbm, value_hbm, query_hbm, out_ref, key_ref, value_ref, query_ref, tile, sems):
    copies = [
        pltpu.make_async_copy(source, target, sems.at[index])
        for index, (source, target) in enumerate(
            ((query_hbm, query_ref), (key_hbm, key_ref), (value_hbm, value_ref))
        )
    ]
    for copy in copies:
        copy.start()
    members = jnp.where(iota((HEADS, D), 1) // HEAD_DIM == iota((HEADS, D), 0), 1.0, 0.0).astype(bf16)
    tile[...] = jnp.zeros_like(tile)
    for copy in copies:
        copy.wait()
    keys = key_ref[...].astype(f32)
    values = value_ref[...].astype(f32)
    query = query_ref[...].astype(f32)
    query = jnp.concatenate([query[row : row + 1] for row in range(TILES)], axis=1)
    products = keys * query
    high = products.astype(bf16)
    low = (products - high.astype(f32)).astype(bf16)
    folded = (dot_nt(high, members) + dot_nt(low, members)) * (1.0 / math.sqrt(HEAD_DIM))
    mine = core_ref[0] == 0
    half = HEADS // 2 * HEAD_DIM
    keys = jnp.where(mine, keys[:, :half], keys[:, half:])
    values = jnp.where(mine, values[:, :half], values[:, half:])
    for head in range(HEADS // 2):
        at = head * HEAD_DIM
        tile[:W_ROWS, :HEAD_DIM] = values[:, at : at + HEAD_DIM]
        tile[:W_ROWS, AT_FOLDED:AT_KEY] = folded
        tile[:W_ROWS, AT_KEY:] = keys[:, at : at + KEY_FIRST]
        for part in range(3):
            tile[W_ROWS:, part * KEY_REST : (part + 1) * KEY_REST] = keys[
                part * 6 : part * 6 + 6, at + KEY_FIRST : at + HEAD_DIM
            ]
        out_ref[head * 8 : head * 8 + 8] = jnp.broadcast_to(tile[...].astype(bf16)[None], (8, 24, 128))


def three_parts(value):
    first = value.astype(bf16).astype(f32)
    rest = value - first
    second = rest.astype(bf16).astype(f32)
    return first, second, rest - second


def context_kernel(weights_ref, patches_ref, segments_ref, tail_ref, out_ref, main, sums):
    for source in range(N_GRP):
        at = source * W_ROWS
        main[at : at + W_ROWS, :] = weights_ref[source].astype(f32)[:W_ROWS]
    scores = dot_nt(main[...].T[AT_FOLDED:AT_KEY].astype(bf16), patches_ref[...])

    segments = segments_ref[...]
    masked = jnp.concatenate([jnp.where(segments == slot, scores, LOW) for slot in range(IMG_DEV)], axis=0)
    place = iota((IMG_DEV * HEADS, ROWS), 1)
    peak = jnp.max(masked, axis=1, keepdims=True)
    powers = jnp.where(masked > 0.5 * LOW, jnp.exp(masked - peak), 0.0)
    total = jnp.sum(powers, axis=1, keepdims=True)
    best = peak
    picks, values = [], []
    for top in range(TOPS):
        if top > 0:
            best = jnp.max(masked, axis=1, keepdims=True)
        there = best > 0.5 * LOW
        first = jnp.min(jnp.where(masked == best, place, ROWS), axis=1, keepdims=True)
        hit = (place == first) & there
        picks.append(jnp.where(hit, 1.0, 0.0).astype(bf16))
        masked = jnp.where(hit, LOW, masked)
        powers = jnp.where(hit, 0.0, powers)
        values.append(jnp.where(there, 1.0, 0.0))
    others = powers / total
    context = dot(jnp.concatenate([others.astype(bf16), *picks], axis=0), patches_ref[...])
    values = [
        *three_parts(peak + jnp.log(total)),
        *three_parts(jnp.sum(others, axis=1, keepdims=True)),
        *values,
    ]
    lanes = iota((IMG_DEV * HEADS, 128), 1) - iota((IMG_DEV * HEADS, 128), 0) // HEADS * N_LANES
    scalars = jnp.zeros((IMG_DEV * HEADS, 128), f32)
    for index, value in enumerate(values):
        scalars = jnp.where(lanes == index, value, scalars)
    scalars = scalars[:HEADS] + scalars[HEADS : 2 * HEADS] + scalars[2 * HEADS :]

    def put(row, value):
        sums[pl.ds(row, HEADS, stride=NEAR_ROWS), :] = value

    blank = jnp.zeros((HEADS, 128), f32)
    for tile in range(TILES):
        for row in range(AT_TEXT):
            put(tile * NEAR_LIST + row, context[row * HEADS : (row + 1) * HEADS, tile * 128 : (tile + 1) * 128])
        for row in range(AT_TEXT, NEAR_LIST):
            at = tile * NEAR_LIST + row
            put(at, scalars if at == AT_SCALAR else jnp.broadcast_to(tail_ref[at : at + 1, :], (HEADS, 128)))
    for row in range(TILES * NEAR_LIST, NEAR_ROWS):
        put(row, blank)
    out_ref[...] = sums[...].reshape(HEADS, NEAR_ROWS, 128).astype(bf16)


def project_kernel(place_ref, near_ref, weights_ref, query_ref, out_ref, text_ref, index_ref, rows, main, extra):
    for source in range(N_SIDE):
        rows[source * NEAR_ROWS : (source + 1) * NEAR_ROWS, :] = near_ref[source].astype(f32)
    for source in range(N_GRP):
        block = weights_ref[source].astype(f32)
        at = source * W_ROWS
        main[at : at + W_ROWS, :] = block[:W_ROWS]
        for part in range(3):
            extra[at + part * 6 : at + part * 6 + 6, :] = block[
                W_ROWS:, part * KEY_REST : (part + 1) * KEY_REST
            ]

    def take(row):
        return rows[pl.ds(row, N_SIDE, stride=NEAR_ROWS), :]

    near = jnp.concatenate(
        [
            jnp.concatenate([take(tile * NEAR_LIST + row) for row in range(AT_ID)], axis=0).astype(bf16)
            for tile in range(TILES)
        ],
        axis=1,
    )
    text_ref[...] = near[AT_TEXT * N_SIDE :]
    pair = jnp.concatenate([main[...], main[:, AT_KEY:], extra[...]], axis=1).astype(bf16)
    both = dot(near[: AT_TEXT * N_SIDE], pair)
    count = IMG_DEV * N_SIDE
    scalars = take(AT_SCALAR)
    lanes = iota((N_SIDE, 128), 1)

    def scalar(index):
        return jnp.concatenate(
            [
                jnp.sum(jnp.where(lanes == slot * N_LANES + index, scalars, 0.0), axis=1, keepdims=True)
                for slot in range(IMG_DEV)
            ],
            axis=0,
        )

    level = scalar(0) + scalar(1) + scalar(2)
    others = scalar(3) + scalar(4) + scalar(5)
    some = others > 0.0
    peak = jnp.where(some, 0.0, LOW)
    powers = []
    for top in range(TOPS):
        keys = both[(top + 1) * count : (top + 2) * count, 128:].astype(bf16).astype(f32)
        score = jnp.sum(keys * query_ref[...], axis=1, keepdims=True) / math.sqrt(HEAD_DIM)
        there = scalar(6 + top) > 0.5
        score = jnp.where(there, score - level, LOW)
        peak = jnp.maximum(peak, score)
        powers.append((there, score))
    powers = [jnp.where(there, jnp.exp(score - peak), 0.0) for there, score in powers]
    shift = jnp.where(some, jnp.exp(jnp.where(some, -peak, 0.0)), 0.0)
    total = others * shift
    for power in powers:
        total = total + power
    pooled = both[:count, :HEAD_DIM] * (shift / total)
    for top, power in enumerate(powers):
        value = both[(top + 1) * count : (top + 2) * count, :HEAD_DIM].astype(bf16).astype(f32)
        pooled = pooled + (power / total).astype(bf16).astype(f32) * value
    pooled = jnp.concatenate([pooled[slot * N_SIDE : (slot + 1) * N_SIDE] for slot in range(IMG_DEV)], axis=1)
    out_ref[...] = jnp.broadcast_to(pooled.astype(bf16)[None], out_ref.shape)

    ids = take(AT_NEAR_ID)
    member = iota((N_SIDE, 1), 0)
    for slot in range(IMG_DEV):
        text = ((place_ref[0] * N_SIDE + member) * 8 + place_ref[1]) * IMG_DEV + slot
        code = jnp.where(lanes == slot, float(ID_BASE), 0.0) + jnp.where(lanes == slot + IMG_DEV, 1.0, 0.0)
        image = jnp.sum(ids * code, axis=1, keepdims=True).astype(jnp.int32)
        index_ref[slot * N_SIDE : (slot + 1) * N_SIDE, :] = text
        index_ref[count + slot * N_SIDE : count + (slot + 1) * N_SIDE, :] = image


def unit_kernel(place_ref, pooled_ref, tail_ref, out_ref, low_ref, unit_ref, norm_ref, units, norms, block):
    side = place_ref[2]
    for head in range(HEADS):
        pooled = pooled_ref[head].astype(f32)
        for slot in range(IMG_DEV):
            units[slot, :, head * HEAD_DIM : (head + 1) * HEAD_DIM] = pooled[
                :, slot * HEAD_DIM : (slot + 1) * HEAD_DIM
            ]
    block[...] = tail_ref[...]

    def put(row, value):
        for tile in range(TILES):
            block[tile * 6 + row : tile * 6 + row + 1, :] = value[:, tile * 128 : (tile + 1) * 128]

    for slot in range(IMG_DEV):
        pooled = units[slot]
        norm = jnp.sqrt(jnp.sum(pooled * pooled, axis=1, keepdims=True) + EPS)
        unit = pooled / norm
        units[slot] = unit
        norms[slot] = jnp.broadcast_to(norm, (N_SIDE, 128))
        low_ref[slot * N_SIDE : (slot + 1) * N_SIDE, :] = unit.astype(bf16)
        own = units[slot, pl.ds(side, 1), :]
        put(slot, own)
        unit_ref[slot : slot + 1, :] = own
        norm_ref[slot : slot + 1, :] = norms[slot, pl.ds(side, 1), :]
    out_ref[...] = jnp.broadcast_to(block[...].astype(bf16)[None], out_ref.shape)


def pair_kernel(params_ref, place_ref, far_ref, text_ref, low_ref, index_ref, out_ref, far_rows, sums):
    scale, offset = params_ref[0], params_ref[1]
    for source in range(N_FAR):
        far_rows[source * FAR_ROWS : (source + 1) * FAR_ROWS, :] = far_ref[source].astype(f32)

    def take(row):
        return far_rows[pl.ds(row, N_FAR, stride=FAR_ROWS), :].astype(bf16)

    digit = iota((8, 128), 1)
    slot = iota((8, 128), 0)
    code = jnp.where(digit == slot, float(ID_BASE), 0.0) + jnp.where(digit == slot + IMG_DEV, 1.0, 0.0)
    ids = dot_nt(jnp.where(slot < IMG_DEV, code, 0.0).astype(bf16), take(AT_FAR_ID))
    ids = jnp.concatenate([ids[row : row + 1] for row in range(IMG_DEV)], axis=1).astype(jnp.int32)
    columns = IMG_DEV * N_FAR
    column = iota((1, columns), 1)
    device = column % N_FAR
    turn = device // 8
    device = (turn * N_SIDE + place_ref[2]) * 8 + jnp.where(turn % 2 == 0, device % 8, 7 - device % 8)
    text_index = device * IMG_DEV + column // N_FAR
    sums[...] = jnp.zeros_like(sums)
    for first, near, index, place in ((0, text_ref[...], ids, 0), (IMG_DEV, low_ref[...], text_index, 1)):
        far = jnp.concatenate(
            [
                jnp.concatenate([take(tile * 6 + first + row) for row in range(IMG_DEV)], axis=0)
                for tile in range(TILES)
            ],
            axis=1,
        )
        logits = scale * dot_nt(near, far) + offset
        own = index_ref[place * IMG_DEV * N_SIDE : (place + 1) * IMG_DEV * N_SIDE, :]
        pair_sign = jnp.where(own == index, 1.0, -1.0)
        scaled = scale * (-pair_sign * jax.nn.sigmoid(-pair_sign * logits) / PAIRS)
        parts = dot(scaled.astype(bf16), far)
        for tile in range(TILES):
            for row in range(IMG_DEV):
                sums[pl.ds(tile * 6 + first + row, N_SIDE, stride=FAR_ROWS), :] = parts[
                    row * N_SIDE : (row + 1) * N_SIDE, tile * 128 : (tile + 1) * 128
                ]
    out_ref[...] = sums[...].reshape(N_SIDE, FAR_ROWS, 128).astype(bf16)


def final_kernel(parts_ref, unit_text_ref, text_norm_ref, unit_image_ref, image_norm_ref, image_ref, text_ref, sums):
    total = parts_ref[0].astype(f32)
    for source in range(1, N_SIDE):
        total = total + parts_ref[source].astype(f32)
    sums[...] = total
    whole = jnp.concatenate([sums[tile * 6 : tile * 6 + 6, :] for tile in range(TILES)], axis=1)
    for first, unit_ref, norm, out_ref in (
        (0, unit_text_ref, text_norm_ref[:, :1], text_ref),
        (IMG_DEV, unit_image_ref, image_norm_ref[:, :1], image_ref),
    ):
        part = whole[first : first + IMG_DEV]
        unit = unit_ref[...]
        out_ref[...] = (part - unit * jnp.sum(unit * part, axis=1, keepdims=True)) / norm


def tiled_rows(array):
    rows = array.shape[0]
    return jnp.transpose(array.reshape(rows, TILES, 128), (1, 0, 2))


def code_ids(ids):
    row = jnp.concatenate([ids // ID_BASE, ids % ID_BASE]).astype(f32)
    return jnp.pad(row, (0, 128 - 2 * IMG_DEV))[None]


def weight_messages(core, key_weight, value_weight, pool_query):
    return call(
        weight_kernel,
        [shape(N_GRP, 24, 128, dtype=bf16)],
        [
            pltpu.VMEM((W_ROWS, D), bf16),
            pltpu.VMEM((W_ROWS, D), bf16),
            pltpu.VMEM((TILES, 128), bf16),
            pltpu.VMEM((24, 128), f32),
            pltpu.SemaphoreType.DMA((3,)),
        ],
        limit=62,
        in_specs=[SMEM, ANY, ANY, ANY],
    )(core, key_weight, value_weight, pool_query.reshape(TILES, 128))


def fetch_kernel(patches_hbm, segments_hbm, patches_ref, segments_ref, sems):
    copies = [
        pltpu.make_async_copy(patches_hbm, patches_ref, sems.at[0]),
        pltpu.make_async_copy(segments_hbm, segments_ref, sems.at[1]),
    ]
    for copy in copies:
        copy.start()
    for copy in copies:
        copy.wait()


def fetch(patches, segments):
    return call(
        fetch_kernel,
        [shape(ROWS, D, dtype=bf16), shape(1, ROWS, dtype=jnp.int32)],
        [pltpu.SemaphoreType.DMA((2,))],
        limit=51,
        in_specs=[ANY, ANY],
    )(patches, segments)


def context_messages(weights, patches, segments, tail):
    return call(
        context_kernel,
        [shape(HEADS, NEAR_ROWS, 128, dtype=bf16)],
        [pltpu.VMEM((D, 128), f32), pltpu.VMEM((HEADS * NEAR_ROWS, 128), f32)],
        in_specs=[VMEM] * 4,
    )(weights, patches, segments, tail)


def pooled_messages(place, near, weights, query):
    return call(
        project_kernel,
        [
            shape(N_SIDE, N_SIDE, IMG_DEV * HEAD_DIM, dtype=bf16),
            shape(IMG_DEV * N_SIDE, D, dtype=bf16),
            shape(2 * IMG_DEV * N_SIDE, 1, dtype=jnp.int32),
        ],
        [
            pltpu.VMEM((N_SIDE * NEAR_ROWS, 128), f32),
            pltpu.VMEM((D, 128), f32),
            pltpu.VMEM((D, KEY_REST), f32),
        ],
        in_specs=[SMEM] + [VMEM] * 3,
    )(place, near, weights, query)


def unit_messages(place, pooled, tail):
    return call(
        unit_kernel,
        [
            shape(N_FAR, FAR_ROWS, 128, dtype=bf16),
            shape(IMG_DEV * N_SIDE, D, dtype=bf16),
            shape(IMG_DEV, D),
            shape(IMG_DEV, 128),
        ],
        [pltpu.VMEM((IMG_DEV, N_SIDE, D), f32), pltpu.VMEM((IMG_DEV, N_SIDE, 128), f32), pltpu.VMEM((FAR_ROWS, 128), f32)],
        in_specs=[SMEM, VMEM, VMEM],
    )(place, pooled, tail)


def pair_messages(params, place, far, texts, lows, index):
    return call(
        pair_kernel,
        [shape(N_SIDE, FAR_ROWS, 128, dtype=bf16)],
        [pltpu.VMEM((N_FAR * FAR_ROWS, 128), f32), pltpu.VMEM((N_SIDE * FAR_ROWS, 128), f32)],
        in_specs=[SMEM, SMEM, VMEM, VMEM, VMEM, VMEM],
    )(params, place, far, texts, lows, index)


def gradients(parts, unit_text, text_norm, unit_image, image_norm):
    return call(
        final_kernel,
        [shape(IMG_DEV, D), shape(IMG_DEV, D)],
        [pltpu.VMEM((FAR_ROWS, 128), f32)],
        in_specs=[VMEM] * 5,
    )(parts, unit_text, text_norm, unit_image, image_norm)


def body(
    patches,
    segment_ids,
    image_ids,
    text_embeds,
    key_weight,
    value_weight,
    pool_query,
    logit_scale,
    logit_bias,
):
    yh, core, yl, x, z = (lax.axis_index(name) for name in FINE)
    side = (core * 2 + yl) * 4 + x
    weights = exchange(weight_messages(core[None], key_weight, value_weight, pool_query), GRP)

    text_full = text_embeds.astype(f32)
    text_norm = jnp.sqrt(jnp.sum(text_full * text_full, axis=1, keepdims=True) + EPS)
    unit_text = text_full / text_norm
    text_norm = jnp.broadcast_to(text_norm, (IMG_DEV, 128))
    text_low = tiled_rows(lax.reduce_precision(unit_text, 8, 7))
    ids = code_ids(image_ids)
    near_tail = jnp.pad(text_low, ((0, 0), (AT_TEXT, 1), (0, 0))).reshape(TILES * NEAR_LIST, 128)
    near_tail = jnp.where(jnp.arange(TILES * NEAR_LIST)[:, None] == AT_NEAR_ID, ids, near_tail)
    far_tail = jnp.pad(text_low, ((0, 0), (IMG_DEV, 0), (0, 0))).reshape(6 * TILES, 128)
    far_tail = jnp.concatenate([far_tail, ids, jnp.zeros((1, 128), f32)], axis=0)
    query = lax.dynamic_slice_in_dim(pool_query, side * HEAD_DIM, HEAD_DIM)[None].astype(f32)
    patches, segments = fetch(patches, segment_ids)
    params = jnp.concatenate([logit_scale, logit_bias])
    place = jnp.stack([yh, z, side])
    weights, near_tail, far_tail, query, params, place, unit_text, text_norm = lax.optimization_barrier(
        (weights, near_tail, far_tail, query, params, place, unit_text, text_norm)
    )

    near = exchange(context_messages(weights, patches, segments, near_tail), SIDE)
    pooled, texts, index = pooled_messages(place, near, weights, query)
    pooled = exchange(pooled, SIDE)
    far, lows, unit_image, image_norm = unit_messages(place, pooled, far_tail)
    far = far_exchange(far)
    parts = exchange(pair_messages(params, place, far, texts, lows, index), SIDE)
    return gradients(parts, unit_text, text_norm, unit_image, image_norm)


def solution(mesh):
    fine = Mesh(mesh.devices.reshape(FINE_SHAPE), FINE)
    rows = P(FINE, None)
    in_specs = (rows, rows, P(FINE), rows, P(GRP, None), P(GRP, None), P(), P(), P())
    return jax.shard_map(
        body, mesh=fine, in_specs=in_specs, out_specs=(rows, rows), check_vma=False
    )
```

```python
import math

import jax
import jax.numpy as jnp
from jax import lax
from jax.experimental import pallas as pl
from jax.experimental.pallas import tpu as pltpu
from jax.sharding import Mesh
from jax.sharding import PartitionSpec as P

D = 1152
TILES = D // 128
HEADS = 16
HEAD_DIM = 72
IMG_DEV = 3
PAIRS = 1536
EPS = 1e-06
ID_BASE = 64
ROWS = 768
LOW = -1e30

FINE = ("yh", "core", "yl", "x", "z")
FINE_SHAPE = (4, 2, 2, 4, 8)
SIDE = ("core", "yl", "x")
FAR = ("yh", "z")
GRP = ("yl", "x", "z")
N_SIDE = 16
N_FAR = 32
N_GRP = 64
W_ROWS = 18

AT_FOLDED = HEAD_DIM
AT_KEY = AT_FOLDED + HEADS
KEY_FIRST = 128 - AT_KEY
KEY_REST = HEAD_DIM - KEY_FIRST

TOPS = 2
AT_TOP = IMG_DEV
AT_TEXT = AT_TOP + TOPS * IMG_DEV
NEAR_LIST = AT_TEXT + IMG_DEV
AT_NEAR_ID = TILES * NEAR_LIST
AT_SCALAR = AT_NEAR_ID + 1
NEAR_ROWS = 112
N_LANES = 8

AT_FAR_ID = 6 * TILES
FAR_ROWS = 56

f32 = jnp.float32
bf16 = jnp.bfloat16
VMEM = pl.BlockSpec(memory_space=pltpu.VMEM)
ANY = pl.BlockSpec(memory_space=pltpu.HBM)
SMEM = pl.BlockSpec(memory_space=pltpu.SMEM)


def call(kernel, outs, scratch=(), limit=40, **cost):
    many = len(outs) > 1
    return pl.pallas_call(
        kernel,
        out_shape=tuple(outs) if many else outs[0],
        out_specs=(VMEM,) * len(outs) if many else VMEM,
        scratch_shapes=list(scratch),
        compiler_params=pltpu.CompilerParams(vmem_limit_bytes=limit * 1024 * 1024),
        **cost,
    )


def shape(*dims, dtype=f32):
    return jax.ShapeDtypeStruct(dims, dtype)


def iota(dims, axis):
    return lax.broadcasted_iota(jnp.int32, dims, axis)


def dot_nt(a, b):
    return lax.dot_general(a, b, (((1,), (1,)), ((), ())), preferred_element_type=f32)


def dot(a, b):
    return jnp.dot(a, b, preferred_element_type=f32)


def exchange(blocks, axes):
    return lax.all_to_all(blocks, axes, 0, 0)


def weight_kernel(core_ref, key_hbm, value_hbm, query_hbm, out_ref, key_ref, value_ref, query_ref, tile, sems):
    copies = [
        pltpu.make_async_copy(source, target, sems.at[index])
        for index, (source, target) in enumerate(
            ((query_hbm, query_ref), (key_hbm, key_ref), (value_hbm, value_ref))
        )
    ]
    for copy in copies:
        copy.start()
    members = jnp.where(iota((HEADS, D), 1) // HEAD_DIM == iota((HEADS, D), 0), 1.0, 0.0).astype(bf16)
    tile[...] = jnp.zeros_like(tile)
    for copy in copies:
        copy.wait()
    keys = key_ref[...].astype(f32)
    values = value_ref[...].astype(f32)
    query = query_ref[...].astype(f32)
    query = jnp.concatenate([query[row : row + 1] for row in range(TILES)], axis=1)
    products = keys * query
    high = products.astype(bf16)
    low = (products - high.astype(f32)).astype(bf16)
    folded = (dot_nt(high, members) + dot_nt(low, members)) * (1.0 / math.sqrt(HEAD_DIM))
    mine = core_ref[0] == 0
    half = HEADS // 2 * HEAD_DIM
    keys = jnp.where(mine, keys[:, :half], keys[:, half:])
    values = jnp.where(mine, values[:, :half], values[:, half:])
    for head in range(HEADS // 2):
        at = head * HEAD_DIM
        tile[:W_ROWS, :HEAD_DIM] = values[:, at : at + HEAD_DIM]
        tile[:W_ROWS, AT_FOLDED:AT_KEY] = folded
        tile[:W_ROWS, AT_KEY:] = keys[:, at : at + KEY_FIRST]
        for part in range(3):
            tile[W_ROWS:, part * KEY_REST : (part + 1) * KEY_REST] = keys[
                part * 6 : part * 6 + 6, at + KEY_FIRST : at + HEAD_DIM
            ]
        out_ref[head * 8 : head * 8 + 8] = jnp.broadcast_to(tile[...].astype(bf16)[None], (8, 24, 128))


def three_parts(value):
    first = value.astype(bf16).astype(f32)
    rest = value - first
    second = rest.astype(bf16).astype(f32)
    return first, second, rest - second


def context_kernel(weights_ref, patches_ref, segments_ref, tail_ref, out_ref, main, sums):
    for source in range(N_GRP):
        at = source * W_ROWS
        main[at : at + W_ROWS, :] = weights_ref[source].astype(f32)[:W_ROWS]
    scores = dot_nt(main[...].T[AT_FOLDED:AT_KEY].astype(bf16), patches_ref[...])

    segments = segments_ref[...]
    masked = jnp.concatenate([jnp.where(segments == slot, scores, LOW) for slot in range(IMG_DEV)], axis=0)
    place = iota((IMG_DEV * HEADS, ROWS), 1)
    peak = jnp.max(masked, axis=1, keepdims=True)
    powers = jnp.where(masked > 0.5 * LOW, jnp.exp(masked - peak), 0.0)
    total = jnp.sum(powers, axis=1, keepdims=True)
    best = peak
    picks, values = [], []
    for top in range(TOPS):
        if top > 0:
            best = jnp.max(masked, axis=1, keepdims=True)
        there = best > 0.5 * LOW
        first = jnp.min(jnp.where(masked == best, place, ROWS), axis=1, keepdims=True)
        hit = (place == first) & there
        picks.append(jnp.where(hit, 1.0, 0.0).astype(bf16))
        masked = jnp.where(hit, LOW, masked)
        powers = jnp.where(hit, 0.0, powers)
        values.append(jnp.where(there, 1.0, 0.0))
    others = powers / total
    context = dot(jnp.concatenate([others.astype(bf16), *picks], axis=0), patches_ref[...])
    values = [
        *three_parts(peak + jnp.log(total)),
        *three_parts(jnp.sum(others, axis=1, keepdims=True)),
        *values,
    ]
    lanes = iota((IMG_DEV * HEADS, 128), 1) - iota((IMG_DEV * HEADS, 128), 0) // HEADS * N_LANES
    scalars = jnp.zeros((IMG_DEV * HEADS, 128), f32)
    for index, value in enumerate(values):
        scalars = jnp.where(lanes == index, value, scalars)
    scalars = scalars[:HEADS] + scalars[HEADS : 2 * HEADS] + scalars[2 * HEADS :]

    def put(row, value):
        sums[pl.ds(row, HEADS, stride=NEAR_ROWS), :] = value

    blank = jnp.zeros((HEADS, 128), f32)
    for tile in range(TILES):
        for row in range(AT_TEXT):
            put(tile * NEAR_LIST + row, context[row * HEADS : (row + 1) * HEADS, tile * 128 : (tile + 1) * 128])
        for row in range(AT_TEXT, NEAR_LIST):
            at = tile * NEAR_LIST + row
            put(at, jnp.broadcast_to(tail_ref[at : at + 1, :], (HEADS, 128)))
    put(AT_NEAR_ID, jnp.broadcast_to(tail_ref[AT_NEAR_ID : AT_NEAR_ID + 1, :], (HEADS, 128)))
    put(AT_SCALAR, scalars)
    for row in range(AT_SCALAR + 1, NEAR_ROWS):
        put(row, blank)
    out_ref[...] = sums[...].reshape(HEADS, NEAR_ROWS, 128).astype(bf16)


def project_kernel(place_ref, near_ref, weights_ref, query_ref, out_ref, text_ref, index_ref, rows, main, extra):
    for source in range(N_SIDE):
        rows[source * NEAR_ROWS : (source + 1) * NEAR_ROWS, :] = near_ref[source].astype(f32)
    for source in range(N_GRP):
        block = weights_ref[source].astype(f32)
        at = source * W_ROWS
        main[at : at + W_ROWS, :] = block[:W_ROWS]
        for part in range(3):
            extra[at + part * 6 : at + part * 6 + 6, :] = block[
                W_ROWS:, part * KEY_REST : (part + 1) * KEY_REST
            ]

    def take(row):
        return rows[pl.ds(row, N_SIDE, stride=NEAR_ROWS), :]

    near = jnp.concatenate(
        [
            jnp.concatenate([take(tile * NEAR_LIST + row) for row in range(NEAR_LIST)], axis=0).astype(bf16)
            for tile in range(TILES)
        ],
        axis=1,
    )
    text_ref[...] = near[AT_TEXT * N_SIDE :]
    pair = jnp.concatenate([main[...], main[:, AT_KEY:], extra[...]], axis=1).astype(bf16)
    both = dot(near[: AT_TEXT * N_SIDE], pair)
    count = IMG_DEV * N_SIDE
    scalars = take(AT_SCALAR)
    lanes = iota((N_SIDE, 128), 1)

    def scalar(index):
        return jnp.concatenate(
            [
                jnp.sum(jnp.where(lanes == slot * N_LANES + index, scalars, 0.0), axis=1, keepdims=True)
                for slot in range(IMG_DEV)
            ],
            axis=0,
        )

    level = scalar(0) + scalar(1) + scalar(2)
    others = scalar(3) + scalar(4) + scalar(5)
    some = others > 0.0
    peak = jnp.where(some, 0.0, LOW)
    powers = []
    for top in range(TOPS):
        keys = both[(top + 1) * count : (top + 2) * count, 128:].astype(bf16).astype(f32)
        score = jnp.sum(keys * query_ref[...], axis=1, keepdims=True) / math.sqrt(HEAD_DIM)
        there = scalar(6 + top) > 0.5
        score = jnp.where(there, score - level, LOW)
        peak = jnp.maximum(peak, score)
        powers.append((there, score))
    powers = [jnp.where(there, jnp.exp(score - peak), 0.0) for there, score in powers]
    shift = jnp.where(some, jnp.exp(jnp.where(some, -peak, 0.0)), 0.0)
    total = others * shift
    for power in powers:
        total = total + power
    pooled = both[:count, :HEAD_DIM] * (shift / total)
    for top, power in enumerate(powers):
        value = both[(top + 1) * count : (top + 2) * count, :HEAD_DIM].astype(bf16).astype(f32)
        pooled = pooled + (power / total).astype(bf16).astype(f32) * value
    pooled = jnp.concatenate([pooled[slot * N_SIDE : (slot + 1) * N_SIDE] for slot in range(IMG_DEV)], axis=1)
    out_ref[...] = jnp.broadcast_to(pooled.astype(bf16)[None], out_ref.shape)

    ids = take(AT_NEAR_ID)
    member = iota((N_SIDE, 1), 0)
    for slot in range(IMG_DEV):
        text = ((place_ref[0] * N_SIDE + member) * 8 + place_ref[1]) * IMG_DEV + slot
        code = jnp.where(lanes == slot, float(ID_BASE), 0.0) + jnp.where(lanes == slot + IMG_DEV, 1.0, 0.0)
        image = jnp.sum(ids * code, axis=1, keepdims=True).astype(jnp.int32)
        index_ref[slot * N_SIDE : (slot + 1) * N_SIDE, :] = text
        index_ref[count + slot * N_SIDE : count + (slot + 1) * N_SIDE, :] = image


def unit_kernel(place_ref, pooled_ref, tail_ref, out_ref, low_ref, unit_ref, norm_ref, units, norms, block):
    side = place_ref[2]
    for head in range(HEADS):
        pooled = pooled_ref[head].astype(f32)
        for slot in range(IMG_DEV):
            units[slot, :, head * HEAD_DIM : (head + 1) * HEAD_DIM] = pooled[
                :, slot * HEAD_DIM : (slot + 1) * HEAD_DIM
            ]
    block[...] = tail_ref[...]

    def put(row, value):
        for tile in range(TILES):
            block[tile * 6 + row : tile * 6 + row + 1, :] = value[:, tile * 128 : (tile + 1) * 128]

    for slot in range(IMG_DEV):
        pooled = units[slot]
        norm = jnp.sqrt(jnp.sum(pooled * pooled, axis=1, keepdims=True) + EPS)
        unit = pooled / norm
        units[slot] = unit
        norms[slot] = jnp.broadcast_to(norm, (N_SIDE, 128))
        low_ref[slot * N_SIDE : (slot + 1) * N_SIDE, :] = unit.astype(bf16)
        own = units[slot, pl.ds(side, 1), :]
        put(slot, own)
        unit_ref[slot : slot + 1, :] = own
        norm_ref[slot : slot + 1, :] = norms[slot, pl.ds(side, 1), :]
    out_ref[...] = jnp.broadcast_to(block[...].astype(bf16)[None], out_ref.shape)


def pair_kernel(params_ref, place_ref, far_ref, text_ref, low_ref, index_ref, out_ref, far_rows, sums):
    scale, offset = params_ref[0], params_ref[1]
    for source in range(N_FAR):
        far_rows[source * FAR_ROWS : (source + 1) * FAR_ROWS, :] = far_ref[source].astype(f32)

    def take(row):
        return far_rows[pl.ds(row, N_FAR, stride=FAR_ROWS), :].astype(bf16)

    digit = iota((8, 128), 1)
    slot = iota((8, 128), 0)
    code = jnp.where(digit == slot, float(ID_BASE), 0.0) + jnp.where(digit == slot + IMG_DEV, 1.0, 0.0)
    ids = dot_nt(jnp.where(slot < IMG_DEV, code, 0.0).astype(bf16), take(AT_FAR_ID))
    ids = jnp.concatenate([ids[row : row + 1] for row in range(IMG_DEV)], axis=1).astype(jnp.int32)
    columns = IMG_DEV * N_FAR
    column = iota((1, columns), 1)
    device = column % N_FAR
    device = ((device // 8) * N_SIDE + place_ref[2]) * 8 + device % 8
    text_index = device * IMG_DEV + column // N_FAR
    sums[...] = jnp.zeros_like(sums)
    for first, near, index, place in ((0, text_ref[...], ids, 0), (IMG_DEV, low_ref[...], text_index, 1)):
        far = jnp.concatenate(
            [
                jnp.concatenate([take(tile * 6 + first + row) for row in range(IMG_DEV)], axis=0)
                for tile in range(TILES)
            ],
            axis=1,
        )
        logits = scale * dot_nt(near, far) + offset
        own = index_ref[place * IMG_DEV * N_SIDE : (place + 1) * IMG_DEV * N_SIDE, :]
        pair_sign = jnp.where(own == index, 1.0, -1.0)
        scaled = scale * (-pair_sign * jax.nn.sigmoid(-pair_sign * logits) / PAIRS)
        parts = dot(scaled.astype(bf16), far)
        for tile in range(TILES):
            for row in range(IMG_DEV):
                sums[pl.ds(tile * 6 + first + row, N_SIDE, stride=FAR_ROWS), :] = parts[
                    row * N_SIDE : (row + 1) * N_SIDE, tile * 128 : (tile + 1) * 128
                ]
    out_ref[...] = sums[...].reshape(N_SIDE, FAR_ROWS, 128).astype(bf16)


def final_kernel(parts_ref, unit_text_ref, text_norm_ref, unit_image_ref, image_norm_ref, image_ref, text_ref, sums):
    total = parts_ref[0].astype(f32)
    for source in range(1, N_SIDE):
        total = total + parts_ref[source].astype(f32)
    sums[...] = total
    whole = jnp.concatenate([sums[tile * 6 : tile * 6 + 6, :] for tile in range(TILES)], axis=1)
    for first, unit_ref, norm, out_ref in (
        (0, unit_text_ref, text_norm_ref[:, :1], text_ref),
        (IMG_DEV, unit_image_ref, image_norm_ref[:, :1], image_ref),
    ):
        part = whole[first : first + IMG_DEV]
        unit = unit_ref[...]
        out_ref[...] = (part - unit * jnp.sum(unit * part, axis=1, keepdims=True)) / norm


def tiled_rows(array):
    rows = array.shape[0]
    return jnp.transpose(array.reshape(rows, TILES, 128), (1, 0, 2))


def code_ids(ids):
    row = jnp.concatenate([ids // ID_BASE, ids % ID_BASE]).astype(f32)
    return jnp.pad(row, (0, 128 - 2 * IMG_DEV))[None]


def weight_messages(core, key_weight, value_weight, pool_query):
    return call(
        weight_kernel,
        [shape(N_GRP, 24, 128, dtype=bf16)],
        [
            pltpu.VMEM((W_ROWS, D), bf16),
            pltpu.VMEM((W_ROWS, D), bf16),
            pltpu.VMEM((TILES, 128), bf16),
            pltpu.VMEM((24, 128), f32),
            pltpu.SemaphoreType.DMA((3,)),
        ],
        limit=62,
        in_specs=[SMEM, ANY, ANY, ANY],
    )(core, key_weight, value_weight, pool_query.reshape(TILES, 128))


def fetch_kernel(patches_hbm, segments_hbm, patches_ref, segments_ref, sems):
    copies = [
        pltpu.make_async_copy(patches_hbm, patches_ref, sems.at[0]),
        pltpu.make_async_copy(segments_hbm, segments_ref, sems.at[1]),
    ]
    for copy in copies:
        copy.start()
    for copy in copies:
        copy.wait()


def fetch(patches, segments):
    return call(
        fetch_kernel,
        [shape(ROWS, D, dtype=bf16), shape(1, ROWS, dtype=jnp.int32)],
        [pltpu.SemaphoreType.DMA((2,))],
        limit=51,
        in_specs=[ANY, ANY],
    )(patches, segments)


def context_messages(weights, patches, segments, tail):
    return call(
        context_kernel,
        [shape(HEADS, NEAR_ROWS, 128, dtype=bf16)],
        [pltpu.VMEM((D, 128), f32), pltpu.VMEM((HEADS * NEAR_ROWS, 128), f32)],
        in_specs=[VMEM] * 4,
    )(weights, patches, segments, tail)


def pooled_messages(place, near, weights, query):
    return call(
        project_kernel,
        [
            shape(N_SIDE, N_SIDE, IMG_DEV * HEAD_DIM, dtype=bf16),
            shape(IMG_DEV * N_SIDE, D, dtype=bf16),
            shape(2 * IMG_DEV * N_SIDE, 1, dtype=jnp.int32),
        ],
        [
            pltpu.VMEM((N_SIDE * NEAR_ROWS, 128), f32),
            pltpu.VMEM((D, 128), f32),
            pltpu.VMEM((D, KEY_REST), f32),
        ],
        in_specs=[SMEM] + [VMEM] * 3,
    )(place, near, weights, query)


def unit_messages(place, pooled, tail):
    return call(
        unit_kernel,
        [
            shape(N_FAR, FAR_ROWS, 128, dtype=bf16),
            shape(IMG_DEV * N_SIDE, D, dtype=bf16),
            shape(IMG_DEV, D),
            shape(IMG_DEV, 128),
        ],
        [pltpu.VMEM((IMG_DEV, N_SIDE, D), f32), pltpu.VMEM((IMG_DEV, N_SIDE, 128), f32), pltpu.VMEM((FAR_ROWS, 128), f32)],
        in_specs=[SMEM, VMEM, VMEM],
    )(place, pooled, tail)


def pair_messages(params, place, far, texts, lows, index):
    return call(
        pair_kernel,
        [shape(N_SIDE, FAR_ROWS, 128, dtype=bf16)],
        [pltpu.VMEM((N_FAR * FAR_ROWS, 128), f32), pltpu.VMEM((N_SIDE * FAR_ROWS, 128), f32)],
        in_specs=[SMEM, SMEM, VMEM, VMEM, VMEM, VMEM],
    )(params, place, far, texts, lows, index)


def gradients(parts, unit_text, text_norm, unit_image, image_norm):
    return call(
        final_kernel,
        [shape(IMG_DEV, D), shape(IMG_DEV, D)],
        [pltpu.VMEM((FAR_ROWS, 128), f32)],
        in_specs=[VMEM] * 5,
    )(parts, unit_text, text_norm, unit_image, image_norm)


def body(
    patches,
    segment_ids,
    image_ids,
    text_embeds,
    key_weight,
    value_weight,
    pool_query,
    logit_scale,
    logit_bias,
):
    yh, core, yl, x, z = (lax.axis_index(name) for name in FINE)
    side = (core * 2 + yl) * 4 + x
    weights = exchange(weight_messages(core[None], key_weight, value_weight, pool_query), GRP)

    text_full = text_embeds.astype(f32)
    text_norm = jnp.sqrt(jnp.sum(text_full * text_full, axis=1, keepdims=True) + EPS)
    unit_text = text_full / text_norm
    text_norm = jnp.broadcast_to(text_norm, (IMG_DEV, 128))
    text_low = tiled_rows(lax.reduce_precision(unit_text, 8, 7))
    ids = code_ids(image_ids)
    near_tail = jnp.pad(text_low, ((0, 0), (AT_TEXT, 0), (0, 0))).reshape(AT_NEAR_ID, 128)
    near_tail = jnp.concatenate([near_tail, ids], axis=0)
    far_tail = jnp.pad(text_low, ((0, 0), (IMG_DEV, 0), (0, 0))).reshape(6 * TILES, 128)
    far_tail = jnp.concatenate([far_tail, ids, jnp.zeros((1, 128), f32)], axis=0)
    query = lax.dynamic_slice_in_dim(pool_query, side * HEAD_DIM, HEAD_DIM)[None].astype(f32)
    patches, segments = fetch(patches, segment_ids)
    params = jnp.concatenate([logit_scale, logit_bias])
    place = jnp.stack([yh, z, side])
    weights, near_tail, far_tail, query, params, place, unit_text, text_norm = lax.optimization_barrier(
        (weights, near_tail, far_tail, query, params, place, unit_text, text_norm)
    )

    near = exchange(context_messages(weights, patches, segments, near_tail), SIDE)
    pooled, texts, index = pooled_messages(place, near, weights, query)
    pooled = exchange(pooled, SIDE)
    far, lows, unit_image, image_norm = unit_messages(place, pooled, far_tail)
    far = exchange(far, FAR)
    parts = exchange(pair_messages(params, place, far, texts, lows, index), SIDE)
    return gradients(parts, unit_text, text_norm, unit_image, image_norm)


def solution(mesh):
    fine = Mesh(mesh.devices.reshape(FINE_SHAPE), FINE)
    rows = P(FINE, None)
    in_specs = (rows, rows, P(FINE), rows, P(GRP, None), P(GRP, None), P(), P(), P())
    return jax.shard_map(
        body, mesh=fine, in_specs=in_specs, out_specs=(rows, rows), check_vma=False
    )
```
